512 devices in a mesh: lat: 8 (over x, core), lon: 64 (over y, z).
Axes of the slice: x: 4, y: 4, z: 16, core: 2. Of those that a mesh axis runs over, the one named last changes fastest.
Arguments:
- rhs: float32 [8, 64, 6, 16, 256], P('lat', 'lon')
- precond: float32 [8, 64, 6, 256], P('lat', 'lon'), may hold values from 0.3 to 1
- factor: bfloat16 [8, 64, 6, 256, 256], P('lat', 'lon')
- kriging: bfloat16 [8, 64, 6, 4, 256, 256], P('lat', 'lon'), may hold values from -0.1875 to 0.1875
- neighbours: int32 [8, 64, 6, 4], P('lat', 'lon'), may hold values from 0 to 3071, as said below
- owner: int32 [3072], replicated, may hold values from 0 to 3071, as said below
- counts: int32 [8, 64], P('lat', 'lon'), may hold values from 1 to 6, as said below
Outputs:
- solution: float32 [8, 64, 6, 16, 256], P('lat', 'lon')
- residual: float32 [8, 64, 6, 16, 256], P('lat', 'lon')
The draws below stay inside these ranges and needn't reach their ends.
Inputs may be any that keep to these rules, and one draw needn't show every extreme that they name: `counts`: each region holds 1 to 6 blocks in its first slots; some region holds 6. `owner`: a permutation of 0 to 3071; block id g lives in slot owner[g] % 6 of region owner[g] // 6. `neighbours`: ids of live blocks in the same region or one of its eight adjacent regions, adjacency periodic in longitude and not in latitude.
All inputs are finite; a program needn't handle non-finite values.
Results may differ from the reference program's by a relative error of at most 0.025.
Values may be sent and summed in bfloat16 or wider, within the bound.
A program may use at most 64 MiB of HBM per device.

```python
import math
import jax
import jax.numpy as jnp
from jax import lax

BLK = 256
NB = 4
SLOTS = 6
SAMPLES = 16
ITERS = 2
NLAT = 8
NLON = 64
BLOCKS = 3072


def layout(key):
    keys = jax.random.split(key, 6)
    regions = NLAT * NLON
    base = jax.random.randint(keys[0], (regions,), 1, SLOTS // 2 + 1)
    dense = jax.random.randint(keys[1], (regions,), 0, 8) == 0
    filled = jnp.where(dense, SLOTS, base)
    chosen = jax.random.randint(keys[2], (), 0, regions)
    filled = filled.at[chosen].set(SLOTS).astype(jnp.int32)
    placing = jax.random.permutation(keys[3], BLOCKS).astype(jnp.int32)
    inverse = jnp.zeros((BLOCKS,), jnp.int32).at[placing].set(jnp.arange(BLOCKS, dtype=jnp.int32))
    code = jax.random.randint(keys[4], (NLAT, NLON, SLOTS, NB), 0, 9)
    row = jnp.arange(NLAT, dtype=jnp.int32)[:, None, None, None]
    col = jnp.arange(NLON, dtype=jnp.int32)[None, :, None, None]
    up = code // 3 - 1
    target_row = row + up
    target_row = jnp.where((target_row < 0) | (target_row >= NLAT), row, target_row)
    target_col = (col + code % 3 - 1) % NLON
    region = target_row * NLON + target_col
    limit = filled[region]
    slot = jax.random.randint(keys[5], (NLAT, NLON, SLOTS, NB), 0, limit)
    ident = inverse[region * SLOTS + slot].astype(jnp.int32)
    return (filled.reshape(NLAT, NLON), placing, ident)


def draw_counts(key, part):
    return layout(key)[0]


def draw_owner(key, part):
    return layout(key)[1]


def draw_neighbours(key, part):
    return layout(key)[2]


def draw_factor(key, part):
    key = jax.random.fold_in(key, 5)
    first, second = jax.random.split(key)
    shape = (NLAT, NLON, SLOTS, BLK, BLK)
    rough = jax.random.normal(first, shape, jnp.float32) * (0.5 / math.sqrt(BLK))
    diag = jax.random.uniform(second, (NLAT, NLON, SLOTS, BLK, 1), jnp.float32, 0.5, 1.5)
    eye = (jnp.arange(BLK)[:, None] == jnp.arange(BLK)[None, :]).astype(jnp.float32)
    return (rough + diag * eye).astype(jnp.bfloat16)


def draw_rhs(key, part):
    key = jax.random.fold_in(key, 11)
    first = jax.random.fold_in(key, 0)
    shape = (NLAT, NLON, SLOTS, SAMPLES, BLK)
    lat_pos = jnp.arange(NLAT, dtype=jnp.float32) / max(NLAT - 1, 1)
    lon_pos = jnp.arange(NLON, dtype=jnp.float32) / (NLON - 1)
    rise = jnp.exp(math.log(3.0) * (lat_pos[:, None] + lon_pos[None, :]) * 0.5)
    values = jax.random.normal(first, shape, jnp.float32)
    return values * rise[:, :, None, None, None]


def level_of(stream_key, dims, cuts, smallest, top_value):
    gain, own = 1.0, jax.random.fold_in(stream_key, 6)
    for dim, blocks in cuts:
        steps = jnp.exp(jax.random.uniform(jax.random.fold_in(own, dim), (blocks,), jnp.float32, smallest / len(cuts), top_value / len(cuts)))
        gain = gain * jnp.repeat(steps, dims[dim] // blocks).reshape([-1 if axis == dim else 1 for axis in range(len(dims))])
    return gain


def bell_draw(key, shape, deviation, reach, shards=(), kind=jnp.bfloat16):
    level = level_of(key, shape, shards, -0.22, 0.18) if shards else 1.0
    drawn = jax.random.normal(key, shape, jnp.float32) * deviation * level
    return jnp.minimum(jnp.maximum(drawn, -reach), reach).astype(kind)


def setup_inputs(seed: int = 0) -> dict:
    splits = jax.random.split(jax.random.key(seed), 8)
    rhs = draw_rhs(jax.random.fold_in(splits[7], 71), 0)
    precond = jnp.clip(jnp.exp(math.log(1.0) - 1.2039728 * jax.random.uniform(splits[1], (NLAT, NLON, SLOTS, BLK), jnp.float32) ** level_of(splits[1], (NLAT, NLON, SLOTS, BLK), ((0, 8), (1, 64)), -0.2, 0.2)), 0.3, 1.0)
    factor = draw_factor(jax.random.fold_in(splits[7], 71), 0)
    kriging = bell_draw(splits[3], (NLAT, NLON, SLOTS, NB, BLK, BLK), (4 * BLK) ** -0.5, 0.1875, ((0, 8), (1, 64)))
    neighbours = draw_neighbours(jax.random.fold_in(splits[7], 71), 0)
    owner = draw_owner(jax.random.fold_in(splits[7], 71), 0)
    counts = draw_counts(jax.random.fold_in(splits[7], 71), 0)
    return {"rhs": rhs, "precond": precond, "factor": factor, "kriging": kriging, "neighbours": neighbours, "owner": owner, "counts": counts}


nugget = 1.0


def inner(first, second):
    return jnp.sum(first * second, axis=(0, 1, 2, 4))


def reference(rhs, precond, factor, kriging, neighbours, owner, counts):
    live = (jnp.arange(SLOTS)[None, None, :] < counts[:, :, None]).astype(jnp.float32)
    source = rhs * live[:, :, :, None, None]
    position = owner[neighbours]
    scaling = precond[:, :, :, None, :]

    def operate(field):
        rounded = field.astype(jnp.bfloat16)
        flat = rounded.reshape(BLOCKS, SAMPLES, BLK)

        def one_row(pieces):
            weights, blocks, where, own, alive = pieces
            panel = flat[where].astype(jnp.float32)
            lifted = own.astype(jnp.float32) - jnp.einsum('lknij,lknsj->lksi', weights.astype(jnp.float32), panel)
            lifted = lifted.astype(jnp.bfloat16).astype(jnp.float32)
            whitened = jnp.einsum('lkij,lksj->lksi', blocks.astype(jnp.float32), lifted) * alive[:, :, None, None]
            whitened = whitened.astype(jnp.bfloat16).astype(jnp.float32)
            back = jnp.einsum('lkji,lksj->lksi', blocks.astype(jnp.float32), whitened)
            back_low = back.astype(jnp.bfloat16).astype(jnp.float32)
            spread = -jnp.einsum('lknji,lksj->lknsi', weights.astype(jnp.float32), back_low)
            return back, spread

        back, spread = lax.map(one_row, (kriging, factor, position, rounded, live))
        summed = jax.ops.segment_sum(spread.reshape(-1, SAMPLES, BLK), position.reshape(-1), num_segments=BLOCKS)
        total = back.reshape(BLOCKS, SAMPLES, BLK) + summed
        return total.reshape(field.shape) + nugget * field

    solution = jnp.zeros_like(source)
    residual = source
    preconditioned = scaling * residual
    direction = preconditioned
    current = inner(residual, preconditioned)
    for step in range(ITERS):
        image = operate(direction)
        alpha = current / inner(direction, image)
        solution = solution + alpha[:, None] * direction
        residual = residual - alpha[:, None] * image
        if step + 1 < ITERS:
            preconditioned = scaling * residual
            following = inner(residual, preconditioned)
            direction = preconditioned + (following / current)[:, None] * direction
            current = following
    return solution, residual
```

```python
import functools

import jax
import jax.numpy as jnp
from jax import lax
from jax.experimental import pallas as pl
from jax.experimental.pallas import tpu as pltpu
from jax.sharding import PartitionSpec as P

ROW = 16
LANES = 128
SMALL = 2.0**-75
NEAR = (0, 1, 2, 3, 5, 6, 7, 8)


def dot(a, b):
    return lax.dot_general(a, b, (((1,), (0,)), ((), ())), preferred_element_type=jnp.float32)


def dot_t(a, b):
    return lax.dot_general(a, b, (((1,), (1,)), ((), ())), preferred_element_type=jnp.float32)


def kernel(
    sizes,
    rhs_hbm, pre_hbm, fac_hbm, kri_hbm, near_ref, owner_ref, count_ref,
    sol_ref, res_ref,
    rhs, pre, fac, kri, lifted, halo, spread, select, out, arrive, row_sum, col_sum,
    load_sem, halo_send, halo_recv, back_send, back_recv, row_send, row_recv, col_send, col_recv,
):
    lats, lons, row = sizes
    slots, samples, width = rhs.shape
    links = kri.shape[1]
    high = slots * samples
    cols = lats * (lons // row)
    lat, lon = lax.axis_index("lat"), lax.axis_index("lon")
    ring, place = lax.rem(lon, row), lax.div(lon, row)
    wide = lons // row
    block = lat * wide + place

    loads = [
        pltpu.make_async_copy(rhs_hbm, rhs, load_sem.at[0]),
        pltpu.make_async_copy(pre_hbm, pre, load_sem.at[1]),
        pltpu.make_async_copy(kri_hbm, kri, load_sem.at[2]),
        pltpu.make_async_copy(fac_hbm, fac, load_sem.at[3]),
    ]
    for load in loads:
        load.start()

    def beside(r):
        up, side = r // 3 - 1, r % 3 - 1
        there = lat + up
        valid = jnp.logical_and(there >= 0, there < lats)
        return valid, (there, lax.rem(lon + side + lons, lons))

    def row_mate(step):
        return (lat, place * row + lax.rem(ring + step, row))

    def col_mate(step):
        other = lax.rem(block + step, cols)
        return (lax.div(other, wide), lax.rem(other, wide) * row + ring)

    def far_first(n):
        return sorted(range(1, n), key=lambda o: -min(o, n - o))

    barrier = pltpu.get_barrier_semaphore()

    def greet(device):
        pl.semaphore_signal(barrier, inc=1, device_id=device, device_id_type=pl.DeviceIdType.MESH)

    for step in far_first(row):
        greet(row_mate(step))
    for step in far_first(cols):
        greet(col_mate(step))
    for r in NEAR:
        valid, device = beside(r)
        pl.when(valid)(functools.partial(greet, device))
    edge = jnp.logical_or(lat == 0, lat == lats - 1)
    around = jnp.where(edge, 5, 8)

    wanted = []
    for b in range(slots):
        for m in range(links):
            position = owner_ref[near_ref[b, m]]
            region = position // slots
            slot = position - region * slots
            region_lat = region // lons
            up = region_lat - lat
            side = lax.rem(region - region_lat * lons - lon + 1 + lons, lons)
            index = ((up + 1) * 3 + side) * slots + slot
            wanted.append(jnp.clip(index, 0, 9 * slots - 1))
    live = [jnp.where(b < count_ref[0, 0], 1.0, 0.0).astype(jnp.float32) for b in range(slots)]

    depth = slots * links * samples
    lane = lax.broadcasted_iota(jnp.int32, (1, depth), 1)
    link, sample = lane // samples, lane % samples
    goal = sample
    for i, w in enumerate(wanted):
        goal = goal + jnp.where(link == i, w * samples, 0)
    for r in range(9):
        rows = lax.broadcasted_iota(jnp.int32, (high, depth), 0) + r * high
        select[r] = jnp.where(rows == goal, 1.0, 0.0).astype(jnp.bfloat16)

    @pl.when(lat == 0)
    def _():
        for k in range(2):
            arrive[k, 0:3] = jnp.zeros((3, high, width), jnp.bfloat16)
            halo[k, 0 : 3 * slots] = jnp.zeros((3 * slots, samples, width), jnp.bfloat16)

    @pl.when(lat == lats - 1)
    def _():
        for k in range(2):
            arrive[k, 6:9] = jnp.zeros((3, high, width), jnp.bfloat16)
            halo[k, 6 * slots : 9 * slots] = jnp.zeros((3 * slots, samples, width), jnp.bfloat16)

    def remote(source, target, send, recv, device):
        return pltpu.make_async_remote_copy(
            src_ref=source, dst_ref=target, send_sem=send, recv_sem=recv,
            device_id=device, device_id_type=pl.DeviceIdType.MESH,
        )

    def halo_copy(k, r):
        valid, device = beside(r)
        copy = remote(
            halo.at[k, pl.ds(4 * slots, slots)], halo.at[k, pl.ds((8 - r) * slots, slots)],
            halo_send.at[k, r], halo_recv.at[k, 8 - r], device,
        )
        return valid, copy

    def halo_arrival(k, r):
        valid, device = beside(r)
        here = halo.at[k, pl.ds(r * slots, slots)]
        return valid, remote(here, here, halo_send.at[k, r], halo_recv.at[k, r], device)

    def back_copy(k, r):
        valid, device = beside(r)
        copy = remote(
            out.at[k, r], arrive.at[k, 8 - r], back_send.at[k, r], back_recv.at[k, 8 - r], device
        )
        return valid, copy

    def back_arrival(k, r):
        valid, device = beside(r)
        here = arrive.at[k, r]
        return valid, remote(here, here, back_send.at[k, r], back_recv.at[k, r], device)

    def send_field(k, parts):
        for b in range(slots):
            halo[k, 4 * slots + b] = parts[b].astype(jnp.bfloat16)
        for r in NEAR:
            valid, copy = halo_copy(k, r)
            pl.when(valid)(copy.start)

    def gather(k):
        for r in NEAR:
            valid, copy = halo_arrival(k, r)
            pl.when(valid)(copy.wait_recv)
        parts = []
        for b in range(slots):
            total = jnp.zeros((samples, width), jnp.float32)
            for m in range(links):
                total = total + dot_t(halo[k, wanted[b * links + m]], kri[b, m])
            parts.append(total)
        return parts

    def whiten(parts):
        return [dot_t(parts[b].astype(jnp.bfloat16), fac[b]) * live[b] for b in range(slots)]

    def send_back(k, white):
        backs = []
        for b in range(slots):
            back = dot(white[b].astype(jnp.bfloat16), fac[b])
            backs.append(back)
            low = back.astype(jnp.bfloat16)
            for m in range(links):
                i = b * links + m
                spread[i * samples : (i + 1) * samples] = (-dot(low, kri[b, m])).astype(jnp.bfloat16)
        terms = spread[...]
        for r in NEAR:
            out[k, r] = dot(select[r], terms).astype(jnp.bfloat16)
            valid, copy = back_copy(k, r)
            pl.when(valid)(copy.start)
        mine = dot(select[4], terms)
        return [backs[b] + mine[b * samples : (b + 1) * samples] for b in range(slots)]

    def take_back(k, parts):
        for r in NEAR:
            valid, copy = back_arrival(k, r)
            pl.when(valid)(copy.wait_recv)
        total = list(parts)
        for r in NEAR:
            for b in range(slots):
                piece = arrive[k, r, b * samples : (b + 1) * samples]
                total[b] = total[b] + piece.astype(jnp.float32)
        return total

    diagonal = lax.broadcasted_iota(jnp.int32, (samples, LANES), 1) - lax.broadcasted_iota(
        jnp.int32, (samples, LANES), 0
    )

    def inner(first, second):
        total = first[0] * second[0]
        for b in range(1, slots):
            total = total + first[b] * second[b]
        return jnp.sum(total, axis=1, keepdims=True)

    def row_copy(k, step):
        here = row_sum.at[k, ring]
        return remote(here, here, row_send.at[k], row_recv.at[k], row_mate(step))

    def col_copy(k, step):
        here = col_sum.at[k, block]
        return remote(here, here, col_send.at[k], col_recv.at[k], col_mate(step))

    def sum_first(k, columns):
        packed = jnp.zeros((samples, LANES), jnp.float32)
        for i, column in enumerate(columns):
            packed = packed + jnp.where(diagonal == i * samples, column, 0.0)
        row_sum[k, ring] = jnp.sum(packed, axis=0, keepdims=True)
        for step in far_first(row):
            row_copy(k, step).start()

    def sum_second(k):
        many = row_sum.at[k, pl.ds(0, row - 1)]
        remote(many, many, row_send.at[k], row_recv.at[k], row_mate(1)).wait_recv()
        col_sum[k, block] = jnp.sum(row_sum[k], axis=0)
        for step in far_first(cols):
            col_copy(k, step).start()

    def sum_last(k, n):
        many = col_sum.at[k, pl.ds(0, cols - 1)]
        remote(many, many, col_send.at[k], col_recv.at[k], col_mate(1)).wait_recv()
        total = jnp.broadcast_to(jnp.sum(col_sum[k], axis=0), (samples, LANES))
        return [
            jnp.sum(jnp.where(diagonal == i * samples, total, 0.0), axis=1, keepdims=True)
            for i in range(n)
        ]

    def sums_sent(k):
        many = row_sum.at[k, pl.ds(0, row - 1)]
        remote(many, many, row_send.at[k], row_recv.at[k], row_mate(1)).wait_send()
        many = col_sum.at[k, pl.ds(0, cols - 1)]
        remote(many, many, col_send.at[k], col_recv.at[k], col_mate(1)).wait_send()

    loads[0].wait()
    loads[1].wait()
    each = range(slots)
    source = [rhs[b] * live[b] for b in each]
    scale = [pre[b : b + 1] for b in each]
    first = [scale[b] * source[b] for b in each]
    pl.semaphore_wait(barrier, row - 1 + cols - 1 + around)
    send_field(0, first)
    loads[2].wait()
    loads[3].wait()

    away = gather(0)
    for b in each:
        lifted[b] = first[b].astype(jnp.bfloat16).astype(jnp.float32) - away[b]
    image = send_back(0, whiten([lifted[b] for b in each]))
    image = take_back(0, image)
    image = [image[b] + first[b] for b in each]

    scaled = [scale[b] * image[b] for b in each]
    less = [SMALL * image[b] for b in each]
    columns = [
        inner(source, first),
        inner(first, image),
        inner(image, scaled),
        inner(less, [SMALL * scaled[b] for b in each]),
    ]
    sum_first(0, columns)
    send_field(1, scaled)
    sum_second(0)
    away = gather(1)
    current, slope, bend, bend_less = sum_last(0, 4)
    alpha = current / slope
    more = alpha * (1.0 / SMALL)
    square = jnp.where(bend < 3e38, (alpha * bend) * alpha, (more * bend_less) * more)
    following = current - 2.0 * alpha * slope + square
    beta = following / current
    second = [(first[b] - alpha * scaled[b]) + beta * first[b] for b in each]
    parts = [
        (1.0 + beta) * lifted[b] - alpha * (scaled[b].astype(jnp.bfloat16).astype(jnp.float32) - away[b])
        for b in each
    ]
    white = whiten(parts)
    sum_first(1, [inner(white, white) + inner(second, second)])
    turned = send_back(1, white)
    residual = [source[b] - alpha * image[b] for b in each]
    sum_second(1)
    turned = take_back(1, turned)
    [slope] = sum_last(1, 1)
    step_size = following / slope
    for b in each:
        sol_ref[b] = alpha * first[b] + step_size * second[b]
        res_ref[b] = residual[b] - step_size * (turned[b] + second[b])

    for k in range(2):
        for r in NEAR:
            valid, copy = halo_copy(k, r)
            pl.when(valid)(copy.wait_send)
            valid, copy = back_copy(k, r)
            pl.when(valid)(copy.wait_send)
        sums_sent(k)


def body(row, rhs, precond, factor, kriging, neighbours, owner, counts):
    slots, links, width = kriging.shape[2], kriging.shape[3], kriging.shape[4]
    samples = rhs.shape[3]
    lats, lons = lax.axis_size("lat"), lax.axis_size("lon")
    cols = lats * (lons // row)
    high = slots * samples
    field = jax.ShapeDtypeStruct((slots, samples, width), jnp.float32)
    anywhere = pl.BlockSpec(memory_space=pl.ANY)
    scalars = pl.BlockSpec(memory_space=pltpu.SMEM)
    vmem = pl.BlockSpec(memory_space=pltpu.VMEM)
    solved, left = pl.pallas_call(
        functools.partial(kernel, (lats, lons, row)),
        out_shape=(field, field),
        in_specs=[anywhere] * 4 + [scalars] * 3,
        out_specs=(vmem, vmem),
        scratch_shapes=[
            pltpu.VMEM((slots, samples, width), jnp.float32),
            pltpu.VMEM((slots, width), jnp.float32),
            pltpu.VMEM((slots, width, width), jnp.bfloat16),
            pltpu.VMEM((slots, links, width, width), jnp.bfloat16),
            pltpu.VMEM((slots, samples, width), jnp.float32),
            pltpu.VMEM((2, 9 * slots, samples, width), jnp.bfloat16),
            pltpu.VMEM((slots * links * samples, width), jnp.bfloat16),
            pltpu.VMEM((9, high, slots * links * samples), jnp.bfloat16),
            pltpu.VMEM((2, 9, high, width), jnp.bfloat16),
            pltpu.VMEM((2, 9, high, width), jnp.bfloat16),
            pltpu.VMEM((2, row, 1, LANES), jnp.float32),
            pltpu.VMEM((2, cols, 1, LANES), jnp.float32),
            pltpu.SemaphoreType.DMA((4,)),
            pltpu.SemaphoreType.DMA((2, 9)),
            pltpu.SemaphoreType.DMA((2, 9)),
            pltpu.SemaphoreType.DMA((2, 9)),
            pltpu.SemaphoreType.DMA((2, 9)),
            pltpu.SemaphoreType.DMA((2,)),
            pltpu.SemaphoreType.DMA((2,)),
            pltpu.SemaphoreType.DMA((2,)),
            pltpu.SemaphoreType.DMA((2,)),
        ],
        compiler_params=pltpu.CompilerParams(
            collective_id=0, has_side_effects=True, vmem_limit_bytes=32 * 2**20
        ),
    )(rhs[0, 0], precond[0, 0], factor[0, 0], kriging[0, 0], neighbours[0, 0], owner, counts)
    return solved[None, None], left[None, None]


def solution(mesh):
    lons = mesh.shape["lon"]
    row = ROW if lons % ROW == 0 else 2
    return jax.shard_map(
        functools.partial(body, row),
        mesh=mesh,
        in_specs=(
            P("lat", "lon", None, None, None),
            P("lat", "lon", None, None),
            P("lat", "lon", None, None, None),
            P("lat", "lon", None, None, None, None),
            P("lat", "lon", None, None),
            P(),
            P("lat", "lon"),
        ),
        out_specs=(P("lat", "lon", None, None, None), P("lat", "lon", None, None, None)),
        check_vma=False,
    )
```

```python
import functools

import jax
import jax.numpy as jnp
from jax import lax
from jax.experimental import pallas as pl
from jax.experimental.pallas import tpu as pltpu
from jax.sharding import PartitionSpec as P

ROW = 16
LANES = 128
NEAR = (3, 5, 0, 2, 6, 8, 1, 7)


def dot(a, b):
    return lax.dot_general(a, b, (((1,), (0,)), ((), ())), preferred_element_type=jnp.float32)


def dot_t(a, b):
    return lax.dot_general(a, b, (((1,), (1,)), ((), ())), preferred_element_type=jnp.float32)


def kernel(
    sizes,
    rhs_hbm, pre_hbm, fac_hbm, kri_hbm, near_hbm, owner_hbm, count_hbm,
    sol_ref, res_ref,
    rhs, pre, fac, kri, near_ref, owner_ref, count_ref, whitened, halo, spread, select, out, arrive, row_sum, col_sum,
    load_sem, halo_send, halo_recv, back_send, back_recv, row_send, row_recv, col_send, col_recv,
):
    lats, lons, row = sizes
    slots, samples, width = rhs.shape
    links = kri.shape[1]
    high = slots * samples
    cols = lats * (lons // row)
    lat, lon = lax.axis_index("lat"), lax.axis_index("lon")
    ring, place = lax.rem(lon, row), lax.div(lon, row)
    wide = lons // row
    block = lat * wide + place

    loads = [
        pltpu.make_async_copy(near_hbm, near_ref, load_sem.at[4]),
        pltpu.make_async_copy(owner_hbm, owner_ref, load_sem.at[5]),
        pltpu.make_async_copy(count_hbm, count_ref, load_sem.at[6]),
        pltpu.make_async_copy(rhs_hbm, rhs, load_sem.at[0]),
        pltpu.make_async_copy(pre_hbm, pre, load_sem.at[1]),
        pltpu.make_async_copy(kri_hbm, kri, load_sem.at[2]),
        pltpu.make_async_copy(fac_hbm, fac, load_sem.at[3]),
    ]
    for load in loads:
        load.start()

    def beside(r):
        up, side = r // 3 - 1, r % 3 - 1
        return lax.rem(lat + up + lats, lats), lax.rem(lon + side + lons, lons)

    def row_mate(step):
        return (lat, place * row + lax.rem(ring + step, row))

    def col_mate(step):
        other = lax.rem(block + step, cols)
        return (lax.div(other, wide), lax.rem(other, wide) * row + ring)

    def far_first(n):
        return sorted(range(1, n), key=lambda o: -min(o, n - o))

    barrier = pltpu.get_barrier_semaphore()

    def greet(device):
        pl.semaphore_signal(barrier, inc=1, device_id=device, device_id_type=pl.DeviceIdType.MESH)

    for r in NEAR:
        greet(beside(r))
    for step in far_first(row):
        greet(row_mate(step))
    for step in far_first(cols):
        greet(col_mate(step))

    for load in loads[:3]:
        load.wait()

    wanted = []
    for b in range(slots):
        for m in range(links):
            position = owner_ref[near_ref[m, b]]
            region = position // slots
            slot = position - region * slots
            region_lat = region // lons
            up = region_lat - lat
            side = lax.rem(region - region_lat * lons - lon + 1 + lons, lons)
            index = ((up + 1) * 3 + side) * slots + slot
            wanted.append(jnp.clip(index, 0, 9 * slots - 1))
    live = [jnp.where(b < count_ref[0, 0], 1.0, 0.0).astype(jnp.float32) for b in range(slots)]

    depth = slots * links * samples
    lane = lax.broadcasted_iota(jnp.int32, (1, depth), 1)
    link, sample = lane // samples, lane % samples
    goal = sample
    for i, w in enumerate(wanted):
        goal = goal + jnp.where(link == i, w * samples, 0)
    for r in range(9):
        rows = lax.broadcasted_iota(jnp.int32, (high, depth), 0) + r * high
        select[r] = jnp.where(rows == goal, 1.0, 0.0).astype(jnp.bfloat16)

    def remote(source, target, send, recv, device):
        return pltpu.make_async_remote_copy(
            src_ref=source, dst_ref=target, send_sem=send, recv_sem=recv,
            device_id=device, device_id_type=pl.DeviceIdType.MESH,
        )

    def halo_copy(k, r):
        return remote(
            halo.at[k, pl.ds(4 * slots, slots)], halo.at[k, pl.ds((8 - r) * slots, slots)],
            halo_send.at[k, r], halo_recv.at[k, 8 - r], beside(r),
        )

    def halo_arrival(k, r):
        here = halo.at[k, pl.ds(r * slots, slots)]
        return remote(here, here, halo_send.at[k, r], halo_recv.at[k, r], beside(r))

    def back_copy(k, r):
        return remote(
            out.at[k, r], arrive.at[k, 8 - r], back_send.at[k, r], back_recv.at[k, 8 - r], beside(r)
        )

    def back_arrival(k, r):
        here = arrive.at[k, r]
        return remote(here, here, back_send.at[k, r], back_recv.at[k, r], beside(r))

    def send_field(k, parts):
        for b in range(slots):
            halo[k, 4 * slots + b] = parts[b].astype(jnp.bfloat16)
        for r in NEAR:
            halo_copy(k, r).start()

    def gather(k):
        for r in NEAR:
            halo_arrival(k, r).wait_recv()
        parts = []
        for b in range(slots):
            total = jnp.zeros((samples, width), jnp.float32)
            for m in range(links):
                total = total + dot_t(halo[k, wanted[b * links + m]], kri[b, m])
            parts.append(total)
        return parts

    def whiten(parts):
        return [dot_t(parts[b].astype(jnp.bfloat16), fac[b]) * live[b] for b in range(slots)]

    def send_back(k, white):
        backs = []
        for b in range(slots):
            back = dot(white[b].astype(jnp.bfloat16), fac[b])
            backs.append(back)
            low = back.astype(jnp.bfloat16)
            for m in range(links):
                i = b * links + m
                spread[i * samples : (i + 1) * samples] = (-dot(low, kri[b, m])).astype(jnp.bfloat16)
        terms = spread[...]
        for r in NEAR:
            out[k, r] = dot(select[r], terms).astype(jnp.bfloat16)
            back_copy(k, r).start()
        mine = dot(select[4], terms)
        return [backs[b] + mine[b * samples : (b + 1) * samples] for b in range(slots)]

    def take_back(k, parts):
        for r in NEAR:
            back_arrival(k, r).wait_recv()
        total = list(parts)
        for r in NEAR:
            for b in range(slots):
                piece = arrive[k, r, b * samples : (b + 1) * samples]
                total[b] = total[b] + piece.astype(jnp.float32)
        return total

    diagonal = lax.broadcasted_iota(jnp.int32, (samples, LANES), 1) - lax.broadcasted_iota(
        jnp.int32, (samples, LANES), 0
    )

    def inner(first, second):
        total = first[0] * second[0]
        for b in range(1, slots):
            total = total + first[b] * second[b]
        return jnp.sum(total, axis=1, keepdims=True)

    def row_copy(k, step):
        here = row_sum.at[k, ring]
        return remote(here, here, row_send.at[k], row_recv.at[k], row_mate(step))

    def col_copy(k, step):
        here = col_sum.at[k, block]
        return remote(here, here, col_send.at[k], col_recv.at[k], col_mate(step))

    def sum_first(k, columns):
        packed = jnp.zeros((samples, LANES), jnp.float32)
        for i, column in enumerate(columns):
            packed = packed + jnp.where(diagonal == i * samples, column, 0.0)
        row_sum[k, ring] = jnp.sum(packed, axis=0, keepdims=True)
        for step in far_first(row):
            row_copy(k, step).start()

    def sum_second(k):
        many = row_sum.at[k, pl.ds(0, row - 1)]
        remote(many, many, row_send.at[k], row_recv.at[k], row_mate(1)).wait_recv()
        col_sum[k, block] = jnp.sum(row_sum[k], axis=0)
        for step in far_first(cols):
            col_copy(k, step).start()

    def sum_last(k, n):
        many = col_sum.at[k, pl.ds(0, cols - 1)]
        remote(many, many, col_send.at[k], col_recv.at[k], col_mate(1)).wait_recv()
        total = jnp.broadcast_to(jnp.sum(col_sum[k], axis=0), (samples, LANES))
        return [
            jnp.sum(jnp.where(diagonal == i * samples, total, 0.0), axis=1, keepdims=True)
            for i in range(n)
        ]

    def sums_sent(k):
        many = row_sum.at[k, pl.ds(0, row - 1)]
        remote(many, many, row_send.at[k], row_recv.at[k], row_mate(1)).wait_send()
        many = col_sum.at[k, pl.ds(0, cols - 1)]
        remote(many, many, col_send.at[k], col_recv.at[k], col_mate(1)).wait_send()

    loads[3].wait()
    loads[4].wait()
    each = range(slots)
    source = [rhs[b] * live[b] for b in each]
    scale = [pre[b] for b in each]
    first = [scale[b] * source[b] for b in each]
    pl.semaphore_wait(barrier, row - 1 + cols - 1 + len(NEAR))
    send_field(0, first)
    loads[5].wait()
    loads[6].wait()

    away = gather(0)
    white = whiten([first[b].astype(jnp.bfloat16).astype(jnp.float32) - away[b] for b in each])
    for b in each:
        whitened[b] = white[b]
    image = send_back(0, white)
    sum_first(0, [inner(source, first), inner(white, white) + inner(first, first)])
    image = take_back(0, image)
    image = [image[b] + first[b] for b in each]

    scaled = [scale[b] * image[b] for b in each]
    send_field(1, scaled)
    slope_seen = inner(first, image)
    sum_second(0)
    away = gather(1)
    current, slope = sum_last(0, 2)
    alpha = current / slope
    parts = [
        alpha * (scaled[b].astype(jnp.bfloat16).astype(jnp.float32) - away[b]) for b in each
    ]
    white = whiten(parts)
    scaled = [alpha * scaled[b] for b in each]
    columns = [
        slope_seen,
        inner([alpha * image[b] for b in each], scaled),
        inner([whitened[b] for b in each], white) + inner(first, scaled),
        inner(white, white) + inner(scaled, scaled),
    ]
    sum_first(1, columns)
    turned = send_back(1, white)
    sum_second(1)
    turned = take_back(1, turned)
    turned = [turned[b] + scaled[b] for b in each]
    slope_seen, bend, mixed, last = sum_last(1, 4)
    following = current - 2.0 * (alpha * slope_seen) + bend
    grown = 1.0 + following / current
    step_size = following / (grown * (grown * slope - 2.0 * mixed) + last)
    along = alpha + step_size * grown
    for b in each:
        sol_ref[b] = along * first[b] - step_size * scaled[b]
        res_ref[b] = source[b] - along * image[b] + step_size * turned[b]

    for k in range(2):
        for r in NEAR:
            halo_copy(k, r).wait_send()
            back_copy(k, r).wait_send()
        sums_sent(k)


def body(row, rhs, precond, factor, kriging, neighbours, owner, counts):
    slots, links, width = kriging.shape[2], kriging.shape[3], kriging.shape[4]
    samples = rhs.shape[3]
    lats, lons = lax.axis_size("lat"), lax.axis_size("lon")
    cols = lats * (lons // row)
    high = slots * samples
    field = jax.ShapeDtypeStruct((slots, samples, width), jnp.float32)
    far = pl.BlockSpec(memory_space=pl.ANY)
    vmem = pl.BlockSpec(memory_space=pltpu.VMEM)
    solved, left = pl.pallas_call(
        functools.partial(kernel, (lats, lons, row)),
        out_shape=(field, field),
        in_specs=[far] * 7,
        out_specs=(vmem, vmem),
        scratch_shapes=[
            pltpu.VMEM((slots, samples, width), jnp.float32),
            pltpu.VMEM((slots, 1, width), jnp.float32),
            pltpu.VMEM((slots, width, width), jnp.bfloat16),
            pltpu.VMEM((slots, links, width, width), jnp.bfloat16),
            pltpu.SMEM((links, slots), jnp.int32),
            pltpu.SMEM(owner.shape, jnp.int32),
            pltpu.SMEM((1, 1), jnp.int32),
            pltpu.VMEM((slots, samples, width), jnp.float32),
            pltpu.VMEM((2, 9 * slots, samples, width), jnp.bfloat16),
            pltpu.VMEM((slots * links * samples, width), jnp.bfloat16),
            pltpu.VMEM((9, high, slots * links * samples), jnp.bfloat16),
            pltpu.VMEM((2, 9, high, width), jnp.bfloat16),
            pltpu.VMEM((2, 9, high, width), jnp.bfloat16),
            pltpu.VMEM((2, row, 1, LANES), jnp.float32),
            pltpu.VMEM((2, cols, 1, LANES), jnp.float32),
            pltpu.SemaphoreType.DMA((7,)),
            pltpu.SemaphoreType.DMA((2, 9)),
            pltpu.SemaphoreType.DMA((2, 9)),
            pltpu.SemaphoreType.DMA((2, 9)),
            pltpu.SemaphoreType.DMA((2, 9)),
            pltpu.SemaphoreType.DMA((2,)),
            pltpu.SemaphoreType.DMA((2,)),
            pltpu.SemaphoreType.DMA((2,)),
            pltpu.SemaphoreType.DMA((2,)),
        ],
        compiler_params=pltpu.CompilerParams(
            collective_id=0, has_side_effects=True, vmem_limit_bytes=32 * 2**20
        ),
    )(
        *(
            pltpu.with_memory_space_constraint(a, pltpu.HBM)
            for a in (
                rhs[0, 0], precond.reshape(slots, 1, width), factor[0, 0], kriging[0, 0],
                neighbours[0, 0].T, owner,
            )
        ),
        counts,
    )
    return solved[None, None], left[None, None]


def solution(mesh):
    lons = mesh.shape["lon"]
    row = ROW if lons % ROW == 0 else 2
    return jax.shard_map(
        functools.partial(body, row),
        mesh=mesh,
        in_specs=(
            P("lat", "lon", None, None, None),
            P("lat", "lon", None, None),
            P("lat", "lon", None, None, None),
            P("lat", "lon", None, None, None, None),
            P("lat", "lon", None, None),
            P(),
            P("lat", "lon"),
        ),
        out_specs=(P("lat", "lon", None, None, None), P("lat", "lon", None, None, None)),
        check_vma=False,
    )
```

```python
import functools

import jax
import jax.numpy as jnp
from jax import lax
from jax.experimental import pallas as pl
from jax.experimental.pallas import tpu as pltpu
from jax.sharding import PartitionSpec as P

ROW = 16
LANES = 128
REACH = 4


def dot(a, b):
    return lax.dot_general(a, b, (((1,), (0,)), ((), ())), preferred_element_type=jnp.float32)


def dot_t(a, b):
    return lax.dot_general(a, b, (((1,), (1,)), ((), ())), preferred_element_type=jnp.float32)


def kernel(
    sizes,
    rhs_hbm, pre_hbm, fac_hbm, kri_hbm, near_hbm, owner_hbm, count_hbm,
    sol_ref, res_ref,
    rhs, pre, fac, kri, near_ref, owner_ref, count_ref, turned_kri, whitened, halo, spread, select,
    out, arrive, relay, row_sum, col_sum,
    load_sem, halo_send, halo_recv, back_send, back_recv,
    relay_send, relay_recv, far_sem, row_send, row_recv, col_send, col_recv,
):
    lats, lons, row = sizes
    slots, samples, width = rhs.shape
    links = kri.shape[1]
    high = slots * samples
    cols = lats * (lons // row)
    lat, lon = lax.axis_index("lat"), lax.axis_index("lon")
    ring, place = lax.rem(lon, row), lax.div(lon, row)
    wide = lons // row
    block = lat * wide + place

    loads = [
        pltpu.make_async_copy(near_hbm, near_ref, load_sem.at[4]),
        pltpu.make_async_copy(owner_hbm, owner_ref, load_sem.at[5]),
        pltpu.make_async_copy(count_hbm, count_ref, load_sem.at[6]),
        pltpu.make_async_copy(rhs_hbm, rhs, load_sem.at[0]),
        pltpu.make_async_copy(pre_hbm, pre, load_sem.at[1]),
        pltpu.make_async_copy(kri_hbm, kri, load_sem.at[2]),
        pltpu.make_async_copy(fac_hbm, fac, load_sem.at[3]),
    ]
    for load in loads:
        load.start()

    def beside(up, side):
        return lax.rem(lat + up + lats, lats), lax.rem(lon + side + lons, lons)

    def at(up, side):
        return (up + 1) * 3 + side + 1

    mate = 1 - 2 * lax.rem(lat, 2)
    near = [(0, -1), (0, 1), (-mate, -1), (-mate, 1), (mate, 0), (-mate, 0)]

    def row_mate(step):
        return (lat, place * row + lax.rem(ring + step, row))

    def col_mate(step):
        other = lax.rem(block + step, cols)
        return (lax.div(other, wide), lax.rem(other, wide) * row + ring)

    def far_first(n):
        return sorted(range(1, n), key=lambda o: -min(o, n - o))

    barrier = pltpu.get_barrier_semaphore()

    def greet(device):
        pl.semaphore_signal(barrier, inc=1, device_id=device, device_id_type=pl.DeviceIdType.MESH)

    close = [step for step in far_first(row) if min(step, row - step) <= REACH]
    for up, side in near:
        greet(beside(up, side))
    for step in close:
        greet(row_mate(step))
    for step in far_first(cols):
        greet(col_mate(step))

    for load in loads[:3]:
        load.wait()

    wanted = []
    for b in range(slots):
        for m in range(links):
            position = owner_ref[near_ref[m, b]]
            region = position // slots
            slot = position - region * slots
            region_lat = region // lons
            up = region_lat - lat
            side = lax.rem(region - region_lat * lons - lon + 1 + lons, lons)
            index = ((up + 1) * 3 + side) * slots + slot
            wanted.append(jnp.clip(index, 0, 9 * slots - 1))
    live = [jnp.where(b < count_ref[0, 0], 1.0, 0.0).astype(jnp.float32) for b in range(slots)]

    depth = slots * links * samples
    lane = lax.broadcasted_iota(jnp.int32, (1, depth), 1)
    link, sample = lane // samples, lane % samples
    goal = sample
    for i, w in enumerate(wanted):
        goal = goal + jnp.where(link == i, w * samples, 0)
    for r in range(9):
        rows = lax.broadcasted_iota(jnp.int32, (high, depth), 0) + r * high
        select[r] = jnp.where(rows == goal, 1.0, 0.0).astype(jnp.bfloat16)

    def remote(source, target, send, recv, device):
        return pltpu.make_async_remote_copy(
            src_ref=source, dst_ref=target, send_sem=send, recv_sem=recv,
            device_id=device, device_id_type=pl.DeviceIdType.MESH,
        )

    def halo_copy(k, up, side):
        own = halo.at[k, pl.ds(4 * slots, slots)]
        there = halo.at[k, pl.ds(at(-up, -side) * slots, slots)]
        send, recv = halo_send.at[k, at(up, side)], halo_recv.at[k, at(-up, -side)]
        return remote(own, there, send, recv, beside(up, side))

    def halo_relay(k, side):
        own = halo.at[k, pl.ds(at(0, side) * slots, slots)]
        there = halo.at[k, pl.ds(at(-mate, side) * slots, slots)]
        send, recv = halo_send.at[k, at(mate, side)], halo_recv.at[k, at(-mate, side)]
        return remote(own, there, send, recv, beside(mate, 0))

    def halo_arrival(k, up, side):
        here = halo.at[k, pl.ds(at(up, side) * slots, slots)]
        send, recv = halo_send.at[k, at(up, side)], halo_recv.at[k, at(up, side)]
        return remote(here, here, send, recv, beside(0, 1))

    def back_copy(k, up, side):
        send, recv = back_send.at[k, at(up, side)], back_recv.at[k, at(-up, -side)]
        own, there = out.at[k, at(up, side)], arrive.at[k, at(-up, -side)]
        return remote(own, there, send, recv, beside(up, side))

    def back_arrival(k, up, side):
        here = arrive.at[k, at(up, side)]
        send, recv = back_send.at[k, at(up, side)], back_recv.at[k, at(up, side)]
        return remote(here, here, send, recv, beside(0, 1))

    def back_relay(k, side):
        i = (side + 1) // 2
        return remote(
            out.at[k, at(mate, side)], relay.at[k, i], relay_send.at[k, i], relay_recv.at[k, i],
            beside(mate, 0),
        )

    def send_field(k, parts):
        for b in range(slots):
            halo[k, 4 * slots + b] = parts[b].astype(jnp.bfloat16)
        for up, side in near:
            halo_copy(k, up, side).start()

    def gather(k):
        for side in (-1, 1):
            halo_arrival(k, 0, side).wait_recv()
            halo_relay(k, side).start()
        for up, side in near[2:] + [(mate, -1), (mate, 1)]:
            halo_arrival(k, up, side).wait_recv()
        parts = []
        for b in range(slots):
            total = jnp.zeros((samples, width), jnp.float32)
            for m in range(links):
                total = total + dot(halo[k, wanted[b * links + m]], turned_kri[b, m])
            parts.append(total)
        return parts

    def whiten(parts):
        return [dot_t(parts[b].astype(jnp.bfloat16), fac[b]) * live[b] for b in range(slots)]

    def send_back(k, white):
        backs = []
        for b in range(slots):
            back = dot(white[b].astype(jnp.bfloat16), fac[b])
            backs.append(back)
            low = back.astype(jnp.bfloat16)
            for m in range(links):
                i = b * links + m
                spread[i * samples : (i + 1) * samples] = (-dot(low, kri[b, m])).astype(jnp.bfloat16)
        terms = spread[...]
        for side in (-1, 1):
            out[k, at(mate, side)] = dot(select[at(mate, side)], terms).astype(jnp.bfloat16)
            back_relay(k, side).start()
        for up, side in near[2:]:
            out[k, at(up, side)] = dot(select[at(up, side)], terms).astype(jnp.bfloat16)
            back_copy(k, up, side).start()
        for side in (-1, 1):
            straight = dot(select[at(0, side)], terms)
            back_relay(k, side).wait_recv()
            both = straight + relay[k, (side + 1) // 2].astype(jnp.float32)
            out[k, at(0, side)] = both.astype(jnp.bfloat16)
            back_copy(k, 0, side).start()
        mine = dot(select[4], terms)
        return [backs[b] + mine[b * samples : (b + 1) * samples] for b in range(slots)]

    def take_back(k, parts):
        for up, side in near:
            back_arrival(k, up, side).wait_recv()
        total = list(parts)
        for up, side in near:
            for b in range(slots):
                piece = arrive[k, at(up, side), b * samples : (b + 1) * samples]
                total[b] = total[b] + piece.astype(jnp.float32)
        return total

    diagonal = lax.broadcasted_iota(jnp.int32, (samples, LANES), 1) - lax.broadcasted_iota(
        jnp.int32, (samples, LANES), 0
    )

    def inner(first, second):
        total = first[0] * second[0]
        for b in range(1, slots):
            total = total + first[b] * second[b]
        return jnp.sum(total, axis=1, keepdims=True)

    def row_copy(k, step):
        here = row_sum.at[k, ring]
        return remote(here, here, row_send.at[k], row_recv.at[k], row_mate(step))

    def col_copy(k, step):
        here = col_sum.at[k, block]
        return remote(here, here, col_send.at[k], col_recv.at[k], col_mate(step))

    def sum_first(k, columns):
        packed = jnp.zeros((samples, LANES), jnp.float32)
        for i, column in enumerate(columns):
            packed = packed + jnp.where(diagonal == i * samples, column, 0.0)
        row_sum[k, ring] = jnp.sum(packed, axis=0, keepdims=True)
        for step in far_first(row):
            row_copy(k, step).start()

    def sum_second(k):
        many = row_sum.at[k, pl.ds(0, row - 1)]
        remote(many, many, row_send.at[k], row_recv.at[k], row_mate(1)).wait_recv()
        col_sum[k, block] = jnp.sum(row_sum[k], axis=0)
        for step in far_first(cols):
            col_copy(k, step).start()

    def sum_last(k, n):
        many = col_sum.at[k, pl.ds(0, cols - 1)]
        remote(many, many, col_send.at[k], col_recv.at[k], col_mate(1)).wait_recv()
        total = jnp.broadcast_to(jnp.sum(col_sum[k], axis=0), (samples, LANES))
        return [
            jnp.sum(jnp.where(diagonal == i * samples, total, 0.0), axis=1, keepdims=True)
            for i in range(n)
        ]

    def sums_sent(k):
        many = row_sum.at[k, pl.ds(0, row - 1)]
        remote(many, many, row_send.at[k], row_recv.at[k], row_mate(1)).wait_send()
        many = col_sum.at[k, pl.ds(0, cols - 1)]
        remote(many, many, col_send.at[k], col_recv.at[k], col_mate(1)).wait_send()

    loads[3].wait()
    loads[4].wait()
    each = range(slots)
    source = [rhs[b] * live[b] for b in each]
    scale = [pre[b] for b in each]
    first = [scale[b] * source[b] for b in each]
    pl.semaphore_wait(barrier, len(near) + len(close) + cols - 1)
    send_field(0, first)
    if len(close) < row - 1:
        for step in (REACH, row - REACH):
            pl.semaphore_signal(
                far_sem, inc=1, device_id=row_mate(step), device_id_type=pl.DeviceIdType.MESH
            )
    loads[5].wait()
    loads[6].wait()
    for b in each:
        for m in range(links):
            turned_kri[b, m] = kri[b, m].T

    away = gather(0)
    white = whiten([first[b].astype(jnp.bfloat16).astype(jnp.float32) - away[b] for b in each])
    for b in each:
        whitened[b] = white[b]
    image = send_back(0, white)
    if len(close) < row - 1:
        pl.semaphore_wait(far_sem, 2)
    sum_first(0, [inner(source, first), inner(white, white) + inner(first, first)])
    image = take_back(0, image)
    image = [image[b] + first[b] for b in each]

    scaled = [scale[b] * image[b] for b in each]
    send_field(1, scaled)
    slope_seen = inner(first, image)
    sum_second(0)
    away = gather(1)
    current, slope = sum_last(0, 2)
    alpha = current / slope
    parts = [
        alpha * (scaled[b].astype(jnp.bfloat16).astype(jnp.float32) - away[b]) for b in each
    ]
    white = whiten(parts)
    scaled = [alpha * scaled[b] for b in each]
    columns = [
        slope_seen,
        inner([alpha * image[b] for b in each], scaled),
        inner([whitened[b] for b in each], white) + inner(first, scaled),
        inner(white, white) + inner(scaled, scaled),
    ]
    sum_first(1, columns)
    turned = send_back(1, white)
    sum_second(1)
    turned = take_back(1, turned)
    turned = [turned[b] + scaled[b] for b in each]
    slope_seen, bend, mixed, last = sum_last(1, 4)
    following = current - 2.0 * (alpha * slope_seen) + bend
    grown = 1.0 + following / current
    step_size = following / (grown * (grown * slope - 2.0 * mixed) + last)
    along = alpha + step_size * grown
    for b in each:
        sol_ref[b] = along * first[b] - step_size * scaled[b]
        res_ref[b] = source[b] - along * image[b] + step_size * turned[b]

    for k in range(2):
        for up, side in near:
            halo_copy(k, up, side).wait_send()
            back_copy(k, up, side).wait_send()
        for side in (-1, 1):
            halo_relay(k, side).wait_send()
            back_relay(k, side).wait_send()
        sums_sent(k)


def body(row, rhs, precond, factor, kriging, neighbours, owner, counts):
    slots, links, width = kriging.shape[2], kriging.shape[3], kriging.shape[4]
    samples = rhs.shape[3]
    lats, lons = lax.axis_size("lat"), lax.axis_size("lon")
    cols = lats * (lons // row)
    high = slots * samples
    field = jax.ShapeDtypeStruct((slots, samples, width), jnp.float32)
    far = pl.BlockSpec(memory_space=pl.ANY)
    vmem = pl.BlockSpec(memory_space=pltpu.VMEM)
    solved, left = pl.pallas_call(
        functools.partial(kernel, (lats, lons, row)),
        out_shape=(field, field),
        in_specs=[far] * 7,
        out_specs=(vmem, vmem),
        scratch_shapes=[
            pltpu.VMEM((slots, samples, width), jnp.float32),
            pltpu.VMEM((slots, 1, width), jnp.float32),
            pltpu.VMEM((slots, width, width), jnp.bfloat16),
            pltpu.VMEM((slots, links, width, width), jnp.bfloat16),
            pltpu.SMEM((links, slots), jnp.int32),
            pltpu.SMEM(owner.shape, jnp.int32),
            pltpu.SMEM((1, 1), jnp.int32),
            pltpu.VMEM((slots, links, width, width), jnp.bfloat16),
            pltpu.VMEM((slots, samples, width), jnp.float32),
            pltpu.VMEM((2, 9 * slots, samples, width), jnp.bfloat16),
            pltpu.VMEM((slots * links * samples, width), jnp.bfloat16),
            pltpu.VMEM((9, high, slots * links * samples), jnp.bfloat16),
            pltpu.VMEM((2, 9, high, width), jnp.bfloat16),
            pltpu.VMEM((2, 9, high, width), jnp.bfloat16),
            pltpu.VMEM((2, 2, high, width), jnp.bfloat16),
            pltpu.VMEM((2, row, 1, LANES), jnp.float32),
            pltpu.VMEM((2, cols, 1, LANES), jnp.float32),
            pltpu.SemaphoreType.DMA((7,)),
            pltpu.SemaphoreType.DMA((2, 9)),
            pltpu.SemaphoreType.DMA((2, 9)),
            pltpu.SemaphoreType.DMA((2, 9)),
            pltpu.SemaphoreType.DMA((2, 9)),
            pltpu.SemaphoreType.DMA((2, 2)),
            pltpu.SemaphoreType.DMA((2, 2)),
            pltpu.SemaphoreType.REGULAR,
            pltpu.SemaphoreType.DMA((2,)),
            pltpu.SemaphoreType.DMA((2,)),
            pltpu.SemaphoreType.DMA((2,)),
            pltpu.SemaphoreType.DMA((2,)),
        ],
        compiler_params=pltpu.CompilerParams(
            collective_id=0, has_side_effects=True, vmem_limit_bytes=32 * 2**20
        ),
    )(
        *(
            pltpu.with_memory_space_constraint(a, pltpu.HBM)
            for a in (
                rhs[0, 0], precond.reshape(slots, 1, width), factor[0, 0], kriging[0, 0],
                neighbours[0, 0].T, owner,
            )
        ),
        counts,
    )
    return solved[None, None], left[None, None]


def solution(mesh):
    lons = mesh.shape["lon"]
    row = ROW if lons % ROW == 0 else 2
    return jax.shard_map(
        functools.partial(body, row),
        mesh=mesh,
        in_specs=(
            P("lat", "lon", None, None, None),
            P("lat", "lon", None, None),
            P("lat", "lon", None, None, None),
            P("lat", "lon", None, None, None, None),
            P("lat", "lon", None, None),
            P(),
            P("lat", "lon"),
        ),
        out_specs=(P("lat", "lon", None, None, None), P("lat", "lon", None, None, None)),
        check_vma=False,
    )
```

```python
import functools

import jax
import jax.numpy as jnp
from jax import lax
from jax.experimental import pallas as pl
from jax.experimental.pallas import tpu as pltpu
from jax.sharding import PartitionSpec as P

ROW = 16
LANES = 128
REACH = 2


def dot(a, b):
    return lax.dot_general(a, b, (((1,), (0,)), ((), ())), preferred_element_type=jnp.float32)


def dot_t(a, b):
    return lax.dot_general(a, b, (((1,), (1,)), ((), ())), preferred_element_type=jnp.float32)


def kernel(
    sizes,
    rhs_hbm, pre_hbm, fac_hbm, kri_hbm, near_hbm, owner_hbm, count_hbm,
    first_ref, scaled_ref, source_ref, image_ref, turned_ref, along_ref, step_ref,
    rhs, pre, fac, kri, near_ref, owner_ref, count_ref, turned_kri, whitened, halo, spread, select,
    out, arrive, relay, row_sum, col_sum,
    load_sem, halo_send, halo_recv, back_send, back_recv,
    relay_send, relay_recv, far_col, far_row, row_send, row_recv, col_send, col_recv,
):
    lats, lons, row = sizes
    slots, samples, width = rhs.shape
    links = kri.shape[1]
    high = slots * samples
    cols = lats * (lons // row)
    lat, lon = lax.axis_index("lat"), lax.axis_index("lon")
    ring, place = lax.rem(lon, row), lax.div(lon, row)
    wide = lons // row
    block = lat * wide + place

    loads = [
        pltpu.make_async_copy(near_hbm, near_ref, load_sem.at[4]),
        pltpu.make_async_copy(owner_hbm, owner_ref, load_sem.at[5]),
        pltpu.make_async_copy(count_hbm, count_ref, load_sem.at[6]),
        pltpu.make_async_copy(rhs_hbm, rhs, load_sem.at[0]),
        pltpu.make_async_copy(pre_hbm, pre, load_sem.at[1]),
        pltpu.make_async_copy(kri_hbm, kri, load_sem.at[2]),
        pltpu.make_async_copy(fac_hbm, fac, load_sem.at[3]),
    ]
    for load in loads:
        load.start()

    def beside(up, side):
        return lax.rem(lat + up + lats, lats), lax.rem(lon + side + lons, lons)

    def at(up, side):
        return (up + 1) * 3 + side + 1

    mate = 1 - 2 * lax.rem(lat, 2)
    near = [(0, -1), (0, 1), (-mate, -1), (-mate, 1), (mate, 0), (-mate, 0)]

    def row_mate(step):
        return (lat, place * row + lax.rem(ring + step, row))

    def col_mate(step):
        other = lax.rem(block + step, cols)
        return (lax.div(other, wide), lax.rem(other, wide) * row + ring)

    def far_first(n):
        return sorted(range(1, n), key=lambda o: -min(o, n - o))

    barrier = pltpu.get_barrier_semaphore()

    def greet(device):
        pl.semaphore_signal(barrier, inc=1, device_id=device, device_id_type=pl.DeviceIdType.MESH)

    handed = lats == 8 and wide == 4 and row == 16
    close = [step for step in far_first(row) if not handed or min(step, row - step) <= REACH]
    mates = [
        (core, x, y)
        for x in range(lats // 2)
        for y in range(wide)
        for core in range(2)
        if core + x + y > 0
        and (not handed or min(x, lats // 2 - x) + min(y, wide - y) <= REACH)
    ]

    def block_mate(core, x, y):
        other = lax.rem(lat % 2 + core, 2) + 2 * lax.rem(lat // 2 + x, lats // 2)
        return other, lax.rem(place + y, wide) * row + ring

    def tell(sem, device):
        pl.semaphore_signal(sem, inc=1, device_id=device, device_id_type=pl.DeviceIdType.MESH)
    for up, side in near:
        greet(beside(up, side))
    for step in close:
        greet(row_mate(step))
    for mate_of in mates:
        greet(block_mate(*mate_of))

    for load in loads[:3]:
        load.wait()

    wanted = []
    for b in range(slots):
        for m in range(links):
            position = owner_ref[near_ref[m, b]]
            region = position // slots
            slot = position - region * slots
            region_lat = region // lons
            up = region_lat - lat
            side = lax.rem(region - region_lat * lons - lon + 1 + lons, lons)
            index = ((up + 1) * 3 + side) * slots + slot
            wanted.append(jnp.clip(index, 0, 9 * slots - 1))
    live = [jnp.where(b < count_ref[0, 0], 1.0, 0.0).astype(jnp.float32) for b in range(slots)]

    depth = slots * links * samples
    lane = lax.broadcasted_iota(jnp.int32, (1, depth), 1)
    link, sample = lane // samples, lane % samples
    goal = sample
    for i, w in enumerate(wanted):
        goal = goal + jnp.where(link == i, w * samples, 0)
    for r in range(9):
        rows = lax.broadcasted_iota(jnp.int32, (high, depth), 0) + r * high
        select[r] = jnp.where(rows == goal, 1.0, 0.0).astype(jnp.bfloat16)

    def remote(source, target, send, recv, device):
        return pltpu.make_async_remote_copy(
            src_ref=source, dst_ref=target, send_sem=send, recv_sem=recv,
            device_id=device, device_id_type=pl.DeviceIdType.MESH,
        )

    def halo_copy(k, up, side):
        own = halo.at[k, pl.ds(4 * slots, slots)]
        there = halo.at[k, pl.ds(at(-up, -side) * slots, slots)]
        send, recv = halo_send.at[k, at(up, side)], halo_recv.at[k, at(-up, -side)]
        return remote(own, there, send, recv, beside(up, side))

    def halo_relay(k, side):
        own = halo.at[k, pl.ds(at(0, side) * slots, slots)]
        there = halo.at[k, pl.ds(at(-mate, side) * slots, slots)]
        send, recv = halo_send.at[k, at(mate, side)], halo_recv.at[k, at(-mate, side)]
        return remote(own, there, send, recv, beside(mate, 0))

    def halo_arrival(k, up, side):
        here = halo.at[k, pl.ds(at(up, side) * slots, slots)]
        send, recv = halo_send.at[k, at(up, side)], halo_recv.at[k, at(up, side)]
        return remote(here, here, send, recv, beside(0, 1))

    def back_copy(k, up, side):
        send, recv = back_send.at[k, at(up, side)], back_recv.at[k, at(-up, -side)]
        own, there = out.at[k, at(up, side)], arrive.at[k, at(-up, -side)]
        return remote(own, there, send, recv, beside(up, side))

    def back_arrival(k, up, side):
        here = arrive.at[k, at(up, side)]
        send, recv = back_send.at[k, at(up, side)], back_recv.at[k, at(up, side)]
        return remote(here, here, send, recv, beside(0, 1))

    def back_relay(k, side):
        i = (side + 1) // 2
        return remote(
            out.at[k, at(mate, side)], relay.at[k, i], relay_send.at[k, i], relay_recv.at[k, i],
            beside(mate, 0),
        )

    def send_field(k, parts):
        for b in range(slots):
            halo[k, 4 * slots + b] = parts[b].astype(jnp.bfloat16)
        for up, side in near:
            halo_copy(k, up, side).start()

    def gather(k):
        for side in (-1, 1):
            halo_arrival(k, 0, side).wait_recv()
            halo_relay(k, side).start()
        for up, side in near[2:] + [(mate, -1), (mate, 1)]:
            halo_arrival(k, up, side).wait_recv()
        parts = []
        for b in range(slots):
            total = jnp.zeros((samples, width), jnp.float32)
            for m in range(links):
                total = total + dot(halo[k, wanted[b * links + m]], turned_kri[b, m])
            parts.append(total)
        return parts

    def whiten(parts):
        return [dot_t(parts[b].astype(jnp.bfloat16), fac[b]) * live[b] for b in range(slots)]

    def send_back(k, white, between=lambda: None):
        backs = []
        for b in range(slots):
            back = dot(white[b].astype(jnp.bfloat16), fac[b])
            backs.append(back)
            low = back.astype(jnp.bfloat16)
            for m in range(links):
                i = b * links + m
                spread[i * samples : (i + 1) * samples] = (-dot(low, kri[b, m])).astype(jnp.bfloat16)
        between()
        terms = spread[...]
        for side in (-1, 1):
            out[k, at(mate, side)] = dot(select[at(mate, side)], terms).astype(jnp.bfloat16)
            back_relay(k, side).start()
        for up, side in near[2:]:
            out[k, at(up, side)] = dot(select[at(up, side)], terms).astype(jnp.bfloat16)
            back_copy(k, up, side).start()
        for side in (-1, 1):
            straight = dot(select[at(0, side)], terms)
            back_relay(k, side).wait_recv()
            both = straight + relay[k, (side + 1) // 2].astype(jnp.float32)
            out[k, at(0, side)] = both.astype(jnp.bfloat16)
            back_copy(k, 0, side).start()
        mine = dot(select[4], terms)
        return [backs[b] + mine[b * samples : (b + 1) * samples] for b in range(slots)]

    def take_back(k, parts):
        for up, side in near:
            back_arrival(k, up, side).wait_recv()
        total = list(parts)
        for up, side in near:
            for b in range(slots):
                piece = arrive[k, at(up, side), b * samples : (b + 1) * samples]
                total[b] = total[b] + piece.astype(jnp.float32)
        return total

    diagonal = lax.broadcasted_iota(jnp.int32, (samples, LANES), 1) - lax.broadcasted_iota(
        jnp.int32, (samples, LANES), 0
    )

    def inner(first, second):
        total = first[0] * second[0]
        for b in range(1, slots):
            total = total + first[b] * second[b]
        return jnp.sum(total, axis=1, keepdims=True)

    def row_copy(k, step):
        here = row_sum.at[k, ring]
        return remote(here, here, row_send.at[k], row_recv.at[k], row_mate(step))

    def col_copy(k, step):
        here = col_sum.at[k, block]
        return remote(here, here, col_send.at[k], col_recv.at[k], col_mate(step))

    def sum_first(k, columns):
        packed = jnp.zeros((samples, LANES), jnp.float32)
        for i, column in enumerate(columns):
            packed = packed + jnp.where(diagonal == i * samples, column, 0.0)
        col_sum[k, block] = jnp.sum(packed, axis=0, keepdims=True)
        for step in far_first(cols):
            col_copy(k, step).start()

    def sum_second(k):
        many = col_sum.at[k, pl.ds(0, cols - 1)]
        remote(many, many, col_send.at[k], col_recv.at[k], col_mate(1)).wait_recv()
        row_sum[k, ring] = jnp.sum(col_sum[k], axis=0)
        for step in far_first(row):
            row_copy(k, step).start()

    def sum_last(k, n):
        many = row_sum.at[k, pl.ds(0, row - 1)]
        remote(many, many, row_send.at[k], row_recv.at[k], row_mate(1)).wait_recv()
        total = jnp.broadcast_to(jnp.sum(row_sum[k], axis=0), (samples, LANES))
        return [
            jnp.sum(jnp.where(diagonal == i * samples, total, 0.0), axis=1, keepdims=True)
            for i in range(n)
        ]

    def sums_sent(k):
        many = row_sum.at[k, pl.ds(0, row - 1)]
        remote(many, many, row_send.at[k], row_recv.at[k], row_mate(1)).wait_send()
        many = col_sum.at[k, pl.ds(0, cols - 1)]
        remote(many, many, col_send.at[k], col_recv.at[k], col_mate(1)).wait_send()

    loads[3].wait()
    loads[4].wait()
    each = range(slots)
    source = [rhs[b] * live[b] for b in each]
    scale = [pre[b] for b in each]
    first = [scale[b] * source[b] for b in each]
    pl.semaphore_wait(barrier, len(near) + len(close) + len(mates))
    send_field(0, first)
    if handed:
        tell(far_col.at[0], block_mate(0, lats // 4, 0))
        tell(far_col.at[0], block_mate(0, 0, wide // 2))
        tell(far_row.at[0], row_mate(REACH))
        tell(far_row.at[0], row_mate(row - REACH))
    loads[5].wait()
    loads[6].wait()
    for b in each:
        for m in range(links):
            turned_kri[b, m] = kri[b, m].T

    away = gather(0)
    if handed:
        pl.semaphore_wait(far_row.at[0], 2)
        tell(far_row.at[1], row_mate(2 * REACH))
        tell(far_row.at[1], row_mate(row - 2 * REACH))
    white = whiten([first[b].astype(jnp.bfloat16).astype(jnp.float32) - away[b] for b in each])
    for b in each:
        whitened[b] = white[b]
    columns = [inner(source, first), inner(white, white) + inner(first, first)]

    def early_sum():
        if handed:
            pl.semaphore_wait(far_col.at[0], 2)
        sum_first(0, columns)

    image = send_back(0, white, early_sum)
    if handed:
        pl.semaphore_wait(far_row.at[1], 2)
    sum_second(0)
    image = take_back(0, image)
    image = [image[b] + first[b] for b in each]

    scaled = [scale[b] * image[b] for b in each]
    send_field(1, scaled)
    slope_seen = inner(first, image)
    away = gather(1)
    current, slope = sum_last(0, 2)
    alpha = current / slope
    parts = [
        alpha * (scaled[b].astype(jnp.bfloat16).astype(jnp.float32) - away[b]) for b in each
    ]
    white = whiten(parts)
    scaled = [alpha * scaled[b] for b in each]
    columns = [
        slope_seen,
        inner([alpha * image[b] for b in each], scaled),
        inner([whitened[b] for b in each], white) + inner(first, scaled),
        inner(white, white) + inner(scaled, scaled),
    ]
    sum_first(1, columns)
    turned = send_back(1, white)
    sum_second(1)
    turned = take_back(1, turned)
    for b in each:
        first_ref[b] = first[b]
        scaled_ref[b] = scaled[b]
        source_ref[b] = source[b]
        image_ref[b] = image[b]
        turned_ref[b] = turned[b] + scaled[b]
    slope_seen, bend, mixed, last = sum_last(1, 4)
    following = current - 2.0 * (alpha * slope_seen) + bend
    grown = 1.0 + following / current
    step_size = following / (grown * (grown * slope - 2.0 * mixed) + last)
    along_ref[...] = jnp.broadcast_to(alpha + step_size * grown, (samples, width))
    step_ref[...] = jnp.broadcast_to(step_size, (samples, width))

    for k in range(2):
        for up, side in near:
            halo_copy(k, up, side).wait_send()
            back_copy(k, up, side).wait_send()
        for side in (-1, 1):
            halo_relay(k, side).wait_send()
            back_relay(k, side).wait_send()
        sums_sent(k)


def body(row, rhs, precond, factor, kriging, neighbours, owner, counts):
    slots, links, width = kriging.shape[2], kriging.shape[3], kriging.shape[4]
    samples = rhs.shape[3]
    lats, lons = lax.axis_size("lat"), lax.axis_size("lon")
    cols = lats * (lons // row)
    high = slots * samples
    field = jax.ShapeDtypeStruct((slots, samples, width), jnp.float32)
    far = pl.BlockSpec(memory_space=pl.ANY)
    vmem = pl.BlockSpec(memory_space=pltpu.VMEM)
    first, scaled, source, image, turned, along, step_size = pl.pallas_call(
        functools.partial(kernel, (lats, lons, row)),
        out_shape=(field,) * 5 + (jax.ShapeDtypeStruct((samples, width), jnp.float32),) * 2,
        in_specs=[far] * 7,
        out_specs=(vmem,) * 7,
        scratch_shapes=[
            pltpu.VMEM((slots, samples, width), jnp.float32),
            pltpu.VMEM((slots, 1, width), jnp.float32),
            pltpu.VMEM((slots, width, width), jnp.bfloat16),
            pltpu.VMEM((slots, links, width, width), jnp.bfloat16),
            pltpu.SMEM((links, slots), jnp.int32),
            pltpu.SMEM(owner.shape, jnp.int32),
            pltpu.SMEM((1, 1), jnp.int32),
            pltpu.VMEM((slots, links, width, width), jnp.bfloat16),
            pltpu.VMEM((slots, samples, width), jnp.float32),
            pltpu.VMEM((2, 9 * slots, samples, width), jnp.bfloat16),
            pltpu.VMEM((slots * links * samples, width), jnp.bfloat16),
            pltpu.VMEM((9, high, slots * links * samples), jnp.bfloat16),
            pltpu.VMEM((2, 9, high, width), jnp.bfloat16),
            pltpu.VMEM((2, 9, high, width), jnp.bfloat16),
            pltpu.VMEM((2, 2, high, width), jnp.bfloat16),
            pltpu.VMEM((2, row, 1, LANES), jnp.float32),
            pltpu.VMEM((2, cols, 1, LANES), jnp.float32),
            pltpu.SemaphoreType.DMA((7,)),
            pltpu.SemaphoreType.DMA((2, 9)),
            pltpu.SemaphoreType.DMA((2, 9)),
            pltpu.SemaphoreType.DMA((2, 9)),
            pltpu.SemaphoreType.DMA((2, 9)),
            pltpu.SemaphoreType.DMA((2, 2)),
            pltpu.SemaphoreType.DMA((2, 2)),
            pltpu.SemaphoreType.REGULAR((1,)),
            pltpu.SemaphoreType.REGULAR((2,)),
            pltpu.SemaphoreType.DMA((2,)),
            pltpu.SemaphoreType.DMA((2,)),
            pltpu.SemaphoreType.DMA((2,)),
            pltpu.SemaphoreType.DMA((2,)),
        ],
        compiler_params=pltpu.CompilerParams(
            collective_id=0, has_side_effects=True, vmem_limit_bytes=32 * 2**20
        ),
    )(
        *(
            pltpu.with_memory_space_constraint(a, pltpu.HBM)
            for a in (
                rhs[0, 0], precond.reshape(slots, 1, width), factor[0, 0], kriging[0, 0],
                neighbours[0, 0].T, owner,
            )
        ),
        counts,
    )
    solved = along * first - step_size * scaled
    left = source - along * image + step_size * turned
    return solved[None, None], left[None, None]


def solution(mesh):
    lons = mesh.shape["lon"]
    row = ROW if lons % ROW == 0 else 2
    return jax.shard_map(
        functools.partial(body, row),
        mesh=mesh,
        in_specs=(
            P("lat", "lon", None, None, None),
            P("lat", "lon", None, None),
            P("lat", "lon", None, None, None),
            P("lat", "lon", None, None, None, None),
            P("lat", "lon", None, None),
            P(),
            P("lat", "lon"),
        ),
        out_specs=(P("lat", "lon", None, None, None), P("lat", "lon", None, None, None)),
        check_vma=False,
    )
```

```python
import functools

import jax
import jax.numpy as jnp
from jax import lax
from jax.experimental import pallas as pl
from jax.experimental.pallas import tpu as pltpu
from jax.sharding import PartitionSpec as P

ROW = 16
LANES = 128
REACH = 2


def dot(a, b):
    return lax.dot_general(a, b, (((1,), (0,)), ((), ())), preferred_element_type=jnp.float32)


def kernel(
    sizes,
    rhs_hbm, pre_hbm, fac_hbm, kri_hbm, near_hbm, owner_hbm, count_hbm,
    first_ref, scaled_ref, source_ref, image_ref, turned_ref, along_ref, step_ref,
    rhs, pre, fac, kri, near_ref, owner_ref, count_ref, turned_kri, turned_fac, whitened, halo, spread, select,
    out, arrive, relay, row_sum, col_sum,
    load_sem, halo_send, halo_recv, back_send, back_recv,
    relay_send, relay_recv, far_col, far_row, row_send, row_recv, col_send, col_recv,
):
    lats, lons, row = sizes
    slots, samples, width = rhs.shape
    links = kri.shape[1]
    high = slots * samples
    cols = lats * (lons // row)
    lat, lon = lax.axis_index("lat"), lax.axis_index("lon")
    ring, place = lax.rem(lon, row), lax.div(lon, row)
    wide = lons // row
    block = lat * wide + place

    loads = [
        pltpu.make_async_copy(count_hbm, count_ref, load_sem.at[0]),
        pltpu.make_async_copy(rhs_hbm, rhs, load_sem.at[1]),
        pltpu.make_async_copy(pre_hbm, pre, load_sem.at[2]),
        pltpu.make_async_copy(near_hbm, near_ref, load_sem.at[3]),
        pltpu.make_async_copy(owner_hbm, owner_ref, load_sem.at[4]),
        pltpu.make_async_copy(kri_hbm, kri, load_sem.at[5]),
        pltpu.make_async_copy(fac_hbm, fac, load_sem.at[6]),
    ]
    for load in loads:
        load.start()

    def beside(up, side):
        return lax.rem(lat + up + lats, lats), lax.rem(lon + side + lons, lons)

    def at(up, side):
        return (up + 1) * 3 + side + 1

    mate = 1 - 2 * lax.rem(lat, 2)
    near = [(0, -1), (0, 1), (-mate, -1), (-mate, 1), (mate, 0), (-mate, 0)]

    def row_mate(step):
        return (lat, place * row + lax.rem(ring + step, row))

    def col_mate(step):
        other = lax.rem(block + step, cols)
        return (lax.div(other, wide), lax.rem(other, wide) * row + ring)

    def far_first(n):
        return sorted(range(1, n), key=lambda o: -min(o, n - o))

    barrier = pltpu.get_barrier_semaphore()

    def greet(device):
        pl.semaphore_signal(barrier, inc=1, device_id=device, device_id_type=pl.DeviceIdType.MESH)

    handed = lats == 8 and wide == 4 and row == 16
    close = [step for step in far_first(row) if not handed or min(step, row - step) <= REACH]
    mates = [
        (core, x, y)
        for x in range(lats // 2)
        for y in range(wide)
        for core in range(2)
        if core + x + y > 0
        and (not handed or min(x, lats // 2 - x) + min(y, wide - y) <= REACH)
    ]

    def block_mate(core, x, y):
        other = lax.rem(lat % 2 + core, 2) + 2 * lax.rem(lat // 2 + x, lats // 2)
        return other, lax.rem(place + y, wide) * row + ring

    def tell(sem, device):
        pl.semaphore_signal(sem, inc=1, device_id=device, device_id_type=pl.DeviceIdType.MESH)
    for up, side in near:
        greet(beside(up, side))
    for step in close:
        greet(row_mate(step))
    for mate_of in mates:
        greet(block_mate(*mate_of))

    def remote(source, target, send, recv, device):
        return pltpu.make_async_remote_copy(
            src_ref=source, dst_ref=target, send_sem=send, recv_sem=recv,
            device_id=device, device_id_type=pl.DeviceIdType.MESH,
        )

    def halo_copy(k, up, side):
        own = halo.at[k, pl.ds(4 * slots, slots)]
        there = halo.at[k, pl.ds(at(-up, -side) * slots, slots)]
        send, recv = halo_send.at[k, at(up, side)], halo_recv.at[k, at(-up, -side)]
        return remote(own, there, send, recv, beside(up, side))

    def halo_relay(k, side):
        own = halo.at[k, pl.ds(at(0, side) * slots, slots)]
        there = halo.at[k, pl.ds(at(-mate, side) * slots, slots)]
        send, recv = halo_send.at[k, at(mate, side)], halo_recv.at[k, at(-mate, side)]
        return remote(own, there, send, recv, beside(mate, 0))

    def halo_arrival(k, up, side):
        here = halo.at[k, pl.ds(at(up, side) * slots, slots)]
        send, recv = halo_send.at[k, at(up, side)], halo_recv.at[k, at(up, side)]
        return remote(here, here, send, recv, beside(0, 1))

    def back_copy(k, up, side):
        send, recv = back_send.at[k, at(up, side)], back_recv.at[k, at(-up, -side)]
        own, there = out.at[k, at(up, side)], arrive.at[k, at(-up, -side)]
        return remote(own, there, send, recv, beside(up, side))

    def back_arrival(k, up, side):
        here = arrive.at[k, at(up, side)]
        send, recv = back_send.at[k, at(up, side)], back_recv.at[k, at(up, side)]
        return remote(here, here, send, recv, beside(0, 1))

    def back_relay(k, side):
        i = (side + 1) // 2
        return remote(
            out.at[k, at(mate, side)], relay.at[k, i], relay_send.at[k, i], relay_recv.at[k, i],
            beside(mate, 0),
        )

    def send_field(k, parts):
        for b in range(slots):
            halo[k, 4 * slots + b] = parts[b].astype(jnp.bfloat16)
        for up, side in near:
            halo_copy(k, up, side).start()

    def gather(k):
        for side in (-1, 1):
            halo_arrival(k, 0, side).wait_recv()
            halo_relay(k, side).start()
        for up, side in near[2:] + [(mate, -1), (mate, 1)]:
            halo_arrival(k, up, side).wait_recv()
        parts = []
        for b in range(slots):
            total = jnp.zeros((samples, width), jnp.float32)
            for m in range(links):
                total = total + dot(halo[k, wanted[b * links + m]], turned_kri[b, m])
            parts.append(total)
        return parts

    def whiten(parts):
        return [dot(parts[b].astype(jnp.bfloat16), turned_fac[b]) * live[b] for b in range(slots)]

    def send_back(k, white, between=lambda: None):
        backs = []
        for b in range(slots):
            back = dot(white[b].astype(jnp.bfloat16), fac[b])
            backs.append(back)
            low = back.astype(jnp.bfloat16)
            for m in range(links):
                i = b * links + m
                spread[i * samples : (i + 1) * samples] = (-dot(low, kri[b, m])).astype(jnp.bfloat16)
        between()
        terms = spread[...]
        for side in (-1, 1):
            out[k, at(mate, side)] = dot(select[at(mate, side)], terms).astype(jnp.bfloat16)
            back_relay(k, side).start()
        for up, side in near[2:]:
            out[k, at(up, side)] = dot(select[at(up, side)], terms).astype(jnp.bfloat16)
            back_copy(k, up, side).start()
        for side in (-1, 1):
            straight = dot(select[at(0, side)], terms)
            back_relay(k, side).wait_recv()
            both = straight + relay[k, (side + 1) // 2].astype(jnp.float32)
            out[k, at(0, side)] = both.astype(jnp.bfloat16)
            back_copy(k, 0, side).start()
        mine = dot(select[4], terms)
        return [backs[b] + mine[b * samples : (b + 1) * samples] for b in range(slots)]

    def take_back(k, parts):
        for up, side in near:
            back_arrival(k, up, side).wait_recv()
        total = list(parts)
        for up, side in near:
            for b in range(slots):
                piece = arrive[k, at(up, side), b * samples : (b + 1) * samples]
                total[b] = total[b] + piece.astype(jnp.float32)
        return total

    diagonal = lax.broadcasted_iota(jnp.int32, (samples, LANES), 1) - lax.broadcasted_iota(
        jnp.int32, (samples, LANES), 0
    )

    def inner(first, second):
        total = first[0] * second[0]
        for b in range(1, slots):
            total = total + first[b] * second[b]
        return jnp.sum(total, axis=1, keepdims=True)

    def row_copy(k, step):
        here = row_sum.at[k, ring]
        return remote(here, here, row_send.at[k], row_recv.at[k], row_mate(step))

    def col_copy(k, step):
        here = col_sum.at[k, block]
        return remote(here, here, col_send.at[k], col_recv.at[k], col_mate(step))

    def sum_first(k, columns):
        packed = jnp.zeros((samples, LANES), jnp.float32)
        for i, column in enumerate(columns):
            packed = packed + jnp.where(diagonal == i * samples, column, 0.0)
        col_sum[k, block] = jnp.sum(packed, axis=0, keepdims=True)
        for step in far_first(cols):
            col_copy(k, step).start()

    def sum_second(k):
        many = col_sum.at[k, pl.ds(0, cols - 1)]
        remote(many, many, col_send.at[k], col_recv.at[k], col_mate(1)).wait_recv()
        row_sum[k, ring] = jnp.sum(col_sum[k], axis=0)
        for step in far_first(row):
            row_copy(k, step).start()

    def sum_last(k, n):
        many = row_sum.at[k, pl.ds(0, row - 1)]
        remote(many, many, row_send.at[k], row_recv.at[k], row_mate(1)).wait_recv()
        total = jnp.broadcast_to(jnp.sum(row_sum[k], axis=0), (samples, LANES))
        return [
            jnp.sum(jnp.where(diagonal == i * samples, total, 0.0), axis=1, keepdims=True)
            for i in range(n)
        ]

    def sums_sent(k):
        many = row_sum.at[k, pl.ds(0, row - 1)]
        remote(many, many, row_send.at[k], row_recv.at[k], row_mate(1)).wait_send()
        many = col_sum.at[k, pl.ds(0, cols - 1)]
        remote(many, many, col_send.at[k], col_recv.at[k], col_mate(1)).wait_send()

    for load in loads[:3]:
        load.wait()
    each = range(slots)
    live = [jnp.where(b < count_ref[0, 0], 1.0, 0.0).astype(jnp.float32) for b in range(slots)]
    source = [rhs[b] * live[b] for b in each]
    scale = [pre[b] for b in each]
    first = [scale[b] * source[b] for b in each]
    pl.semaphore_wait(barrier, len(near) + len(close) + len(mates))
    send_field(0, first)
    if handed:
        tell(far_col.at[0], block_mate(0, lats // 4, 0))
        tell(far_col.at[0], block_mate(0, 0, wide // 2))
        tell(far_row.at[0], row_mate(REACH))
        tell(far_row.at[0], row_mate(row - REACH))

    loads[3].wait()
    loads[4].wait()

    wanted = []
    for b in range(slots):
        for m in range(links):
            position = owner_ref[near_ref[m, b]]
            region = position // slots
            slot = position - region * slots
            region_lat = region // lons
            up = region_lat - lat
            side = lax.rem(region - region_lat * lons - lon + 1 + lons, lons)
            index = ((up + 1) * 3 + side) * slots + slot
            wanted.append(jnp.clip(index, 0, 9 * slots - 1))
    depth = slots * links * samples
    lane = lax.broadcasted_iota(jnp.int32, (1, depth), 1)
    link, sample = lane // samples, lane % samples
    goal = sample
    for i, w in enumerate(wanted):
        goal = goal + jnp.where(link == i, w * samples, 0)
    for r in range(9):
        rows = lax.broadcasted_iota(jnp.int32, (high, depth), 0) + r * high
        select[r] = jnp.where(rows == goal, 1.0, 0.0).astype(jnp.bfloat16)

    loads[5].wait()
    for b in each:
        for m in range(links):
            turned_kri[b, m] = kri[b, m].T
    loads[6].wait()
    for b in each:
        turned_fac[b] = fac[b].T

    away = gather(0)
    if handed:
        pl.semaphore_wait(far_row.at[0], 2)
        tell(far_row.at[1], row_mate(2 * REACH))
        tell(far_row.at[1], row_mate(row - 2 * REACH))
    white = whiten([first[b].astype(jnp.bfloat16).astype(jnp.float32) - away[b] for b in each])
    for b in each:
        whitened[b] = white[b]
    columns = [inner(source, first), inner(white, white) + inner(first, first)]

    def early_sum():
        if handed:
            pl.semaphore_wait(far_col.at[0], 2)
        sum_first(0, columns)

    image = send_back(0, white, early_sum)
    if handed:
        pl.semaphore_wait(far_row.at[1], 2)
    sum_second(0)
    image = take_back(0, image)
    image = [image[b] + first[b] for b in each]

    scaled = [scale[b] * image[b] for b in each]
    send_field(1, scaled)
    slope_seen = inner(first, image)
    away = gather(1)
    current, slope = sum_last(0, 2)
    alpha = current / slope
    parts = [
        alpha * (scaled[b].astype(jnp.bfloat16).astype(jnp.float32) - away[b]) for b in each
    ]
    white = whiten(parts)
    scaled = [alpha * scaled[b] for b in each]
    even = [alpha * white[b] for b in each]
    less = [alpha * scaled[b] for b in each]
    columns = [
        slope_seen,
        inner([alpha * image[b] for b in each], scaled),
        inner([whitened[b] for b in each], even) + inner(first, less),
        inner(white, even) + inner(scaled, less),
    ]
    sum_first(1, columns)
    turned = send_back(1, white)
    sum_second(1)
    turned = take_back(1, turned)
    for b in each:
        first_ref[b] = first[b]
        scaled_ref[b] = scaled[b]
        source_ref[b] = source[b]
        image_ref[b] = image[b]
        turned_ref[b] = turned[b] + scaled[b]
    for k in range(2):
        for up, side in near:
            halo_copy(k, up, side).wait_send()
            back_copy(k, up, side).wait_send()
        for side in (-1, 1):
            halo_relay(k, side).wait_send()
            back_relay(k, side).wait_send()
    sums_sent(0)
    slope_seen, bend, mixed, last = sum_last(1, 4)
    following = current - 2.0 * (alpha * slope_seen) + bend
    grown = 1.0 + following / current
    step_size = alpha * (following / (grown * (grown * current - 2.0 * mixed) + last))
    along_ref[...] = jnp.broadcast_to(alpha + step_size * grown, (samples, width))
    step_ref[...] = jnp.broadcast_to(step_size, (samples, width))
    sums_sent(1)


def body(row, rhs, precond, factor, kriging, neighbours, owner, counts):
    slots, links, width = kriging.shape[2], kriging.shape[3], kriging.shape[4]
    samples = rhs.shape[3]
    lats, lons = lax.axis_size("lat"), lax.axis_size("lon")
    cols = lats * (lons // row)
    high = slots * samples
    field = jax.ShapeDtypeStruct((slots, samples, width), jnp.float32)
    far = pl.BlockSpec(memory_space=pl.ANY)
    vmem = pl.BlockSpec(memory_space=pltpu.VMEM)
    first, scaled, source, image, turned, along, step_size = pl.pallas_call(
        functools.partial(kernel, (lats, lons, row)),
        out_shape=(field,) * 5 + (jax.ShapeDtypeStruct((samples, width), jnp.float32),) * 2,
        in_specs=[far] * 7,
        out_specs=(vmem,) * 7,
        scratch_shapes=[
            pltpu.VMEM((slots, samples, width), jnp.float32),
            pltpu.VMEM((slots, 1, width), jnp.float32),
            pltpu.VMEM((slots, width, width), jnp.bfloat16),
            pltpu.VMEM((slots, links, width, width), jnp.bfloat16),
            pltpu.SMEM((links, slots), jnp.int32),
            pltpu.SMEM(owner.shape, jnp.int32),
            pltpu.SMEM((1, 1), jnp.int32),
            pltpu.VMEM((slots, links, width, width), jnp.bfloat16),
            pltpu.VMEM((slots, width, width), jnp.bfloat16),
            pltpu.VMEM((slots, samples, width), jnp.float32),
            pltpu.VMEM((2, 9 * slots, samples, width), jnp.bfloat16),
            pltpu.VMEM((slots * links * samples, width), jnp.bfloat16),
            pltpu.VMEM((9, high, slots * links * samples), jnp.bfloat16),
            pltpu.VMEM((2, 9, high, width), jnp.bfloat16),
            pltpu.VMEM((2, 9, high, width), jnp.bfloat16),
            pltpu.VMEM((2, 2, high, width), jnp.bfloat16),
            pltpu.VMEM((2, row, 1, LANES), jnp.float32),
            pltpu.VMEM((2, cols, 1, LANES), jnp.float32),
            pltpu.SemaphoreType.DMA((7,)),
            pltpu.SemaphoreType.DMA((2, 9)),
            pltpu.SemaphoreType.DMA((2, 9)),
            pltpu.SemaphoreType.DMA((2, 9)),
            pltpu.SemaphoreType.DMA((2, 9)),
            pltpu.SemaphoreType.DMA((2, 2)),
            pltpu.SemaphoreType.DMA((2, 2)),
            pltpu.SemaphoreType.REGULAR((1,)),
            pltpu.SemaphoreType.REGULAR((2,)),
            pltpu.SemaphoreType.DMA((2,)),
            pltpu.SemaphoreType.DMA((2,)),
            pltpu.SemaphoreType.DMA((2,)),
            pltpu.SemaphoreType.DMA((2,)),
        ],
        compiler_params=pltpu.CompilerParams(
            collective_id=0, has_side_effects=True, vmem_limit_bytes=32 * 2**20
        ),
    )(
        *(
            pltpu.with_memory_space_constraint(a, pltpu.HBM)
            for a in (
                rhs[0, 0], precond.reshape(slots, 1, width), factor[0, 0], kriging[0, 0],
                neighbours[0, 0].T, owner,
            )
        ),
        counts,
    )
    solved = along * first - step_size * scaled
    left = source - along * image + step_size * turned
    return solved[None, None], left[None, None]


def solution(mesh):
    lons = mesh.shape["lon"]
    row = ROW if lons % ROW == 0 else 2
    return jax.shard_map(
        functools.partial(body, row),
        mesh=mesh,
        in_specs=(
            P("lat", "lon", None, None, None),
            P("lat", "lon", None, None),
            P("lat", "lon", None, None, None),
            P("lat", "lon", None, None, None, None),
            P("lat", "lon", None, None),
            P(),
            P("lat", "lon"),
        ),
        out_specs=(P("lat", "lon", None, None, None), P("lat", "lon", None, None, None)),
        check_vma=False,
    )
```

```python
import functools

import jax
import jax.numpy as jnp
from jax import lax
from jax.experimental import pallas as pl
from jax.experimental.pallas import tpu as pltpu
from jax.sharding import PartitionSpec as P

ROW = 16
LANES = 128
REACH = 2


def dot(a, b):
    return lax.dot_general(a, b, (((1,), (0,)), ((), ())), preferred_element_type=jnp.float32)


def kernel(
    sizes,
    rhs_hbm, pre_hbm, fac_hbm, kri_hbm, near_hbm, owner_hbm, count_hbm,
    first_ref, scaled_ref, source_ref, image_ref, turned_ref, along_ref, step_ref,
    rhs, pre, fac, kri, near_ref, owner_ref, count_ref, turned_kri, turned_fac, whitened, halo, spread, select,
    out, arrive, relay, row_sum, col_sum,
    load_sem, halo_send, halo_recv, back_send, back_recv,
    relay_send, relay_recv, far_col, far_row, row_send, row_recv, col_send, col_recv,
):
    lats, lons, row = sizes
    slots, samples, width = rhs.shape
    links = kri.shape[1]
    high = slots * samples
    cols = lats * (lons // row)
    lat, lon = lax.axis_index("lat"), lax.axis_index("lon")
    ring, place = lax.rem(lon, row), lax.div(lon, row)
    wide = lons // row
    block = lat * wide + place

    loads = [
        pltpu.make_async_copy(count_hbm, count_ref, load_sem.at[0]),
        pltpu.make_async_copy(rhs_hbm, rhs, load_sem.at[1]),
        pltpu.make_async_copy(pre_hbm, pre, load_sem.at[2]),
        pltpu.make_async_copy(near_hbm, near_ref, load_sem.at[3]),
        pltpu.make_async_copy(owner_hbm, owner_ref, load_sem.at[4]),
        pltpu.make_async_copy(kri_hbm, kri, load_sem.at[5]),
        pltpu.make_async_copy(fac_hbm, fac, load_sem.at[6]),
    ]
    for load in loads:
        load.start()

    def beside(up, side):
        return lax.rem(lat + up + lats, lats), lax.rem(lon + side + lons, lons)

    def at(up, side):
        return (up + 1) * 3 + side + 1

    mate = 1 - 2 * lax.rem(lat, 2)
    near = [(0, -1), (0, 1), (-mate, -1), (-mate, 1), (mate, 0), (-mate, 0)]

    def row_mate(step):
        return (lat, place * row + lax.rem(ring + step, row))

    def col_mate(step):
        other = lax.rem(block + step, cols)
        return (lax.div(other, wide), lax.rem(other, wide) * row + ring)

    def far_first(n):
        return sorted(range(1, n), key=lambda o: -min(o, n - o))

    barrier = pltpu.get_barrier_semaphore()

    def greet(device):
        pl.semaphore_signal(barrier, inc=1, device_id=device, device_id_type=pl.DeviceIdType.MESH)

    handed = lats == 8 and wide == 4 and row == 16
    close = [step for step in far_first(row) if not handed or min(step, row - step) <= REACH]
    mates = [
        (core, x, y)
        for x in range(lats // 2)
        for y in range(wide)
        for core in range(2)
        if core + x + y > 0
        and (not handed or min(x, lats // 2 - x) + min(y, wide - y) <= REACH)
    ]

    def block_mate(core, x, y):
        other = lax.rem(lat % 2 + core, 2) + 2 * lax.rem(lat // 2 + x, lats // 2)
        return other, lax.rem(place + y, wide) * row + ring

    def tell(sem, device):
        pl.semaphore_signal(sem, inc=1, device_id=device, device_id_type=pl.DeviceIdType.MESH)
    for up, side in near:
        greet(beside(up, side))
    for step in close:
        greet(row_mate(step))
    for mate_of in mates:
        greet(block_mate(*mate_of))

    def remote(source, target, send, recv, device):
        return pltpu.make_async_remote_copy(
            src_ref=source, dst_ref=target, send_sem=send, recv_sem=recv,
            device_id=device, device_id_type=pl.DeviceIdType.MESH,
        )

    def halo_copy(k, up, side):
        own = halo.at[k, pl.ds(4 * slots, slots)]
        there = halo.at[k, pl.ds(at(-up, -side) * slots, slots)]
        send, recv = halo_send.at[k, at(up, side)], halo_recv.at[k, at(-up, -side)]
        return remote(own, there, send, recv, beside(up, side))

    def halo_relay(k, side):
        own = halo.at[k, pl.ds(at(0, side) * slots, slots)]
        there = halo.at[k, pl.ds(at(-mate, side) * slots, slots)]
        send, recv = halo_send.at[k, at(mate, side)], halo_recv.at[k, at(-mate, side)]
        return remote(own, there, send, recv, beside(mate, 0))

    def halo_arrival(k, up, side):
        here = halo.at[k, pl.ds(at(up, side) * slots, slots)]
        send, recv = halo_send.at[k, at(up, side)], halo_recv.at[k, at(up, side)]
        return remote(here, here, send, recv, beside(0, 1))

    def back_copy(k, up, side):
        send, recv = back_send.at[k, at(up, side)], back_recv.at[k, at(-up, -side)]
        own, there = out.at[k, at(up, side)], arrive.at[k, at(-up, -side)]
        return remote(own, there, send, recv, beside(up, side))

    def back_arrival(k, up, side):
        here = arrive.at[k, at(up, side)]
        send, recv = back_send.at[k, at(up, side)], back_recv.at[k, at(up, side)]
        return remote(here, here, send, recv, beside(0, 1))

    def back_relay(k, side):
        i = (side + 1) // 2
        return remote(
            out.at[k, at(mate, side)], relay.at[k, i], relay_send.at[k, i], relay_recv.at[k, i],
            beside(mate, 0),
        )

    def send_field(k, parts):
        for b in range(slots):
            halo[k, 4 * slots + b] = parts[b].astype(jnp.bfloat16)
        for up, side in near:
            halo_copy(k, up, side).start()

    def gather(k):
        for side in (-1, 1):
            halo_arrival(k, 0, side).wait_recv()
            halo_relay(k, side).start()
        for up, side in near[2:] + [(mate, -1), (mate, 1)]:
            halo_arrival(k, up, side).wait_recv()
        parts = []
        for b in range(slots):
            total = jnp.zeros((samples, width), jnp.float32)
            for m in range(links):
                total = total + dot(halo[k, wanted[b * links + m]], turned_kri[b, m])
            parts.append(total)
        return parts

    def whiten(parts):
        return [dot(parts[b].astype(jnp.bfloat16), turned_fac[b]) * live[b] for b in range(slots)]

    def send_back(k, white, between=lambda: None):
        backs = []
        for b in range(slots):
            back = dot(white[b].astype(jnp.bfloat16), fac[b])
            backs.append(back)
            low = back.astype(jnp.bfloat16)
            for m in range(links):
                i = b * links + m
                spread[i * samples : (i + 1) * samples] = (-dot(low, kri[b, m])).astype(jnp.bfloat16)
        between()
        terms = spread[...]
        for side in (-1, 1):
            out[k, at(mate, side)] = dot(select[at(mate, side)], terms).astype(jnp.bfloat16)
            back_relay(k, side).start()
        for up, side in near[2:]:
            out[k, at(up, side)] = dot(select[at(up, side)], terms).astype(jnp.bfloat16)
            back_copy(k, up, side).start()
        for side in (-1, 1):
            straight = dot(select[at(0, side)], terms)
            back_relay(k, side).wait_recv()
            both = straight + relay[k, (side + 1) // 2].astype(jnp.float32)
            out[k, at(0, side)] = both.astype(jnp.bfloat16)
            back_copy(k, 0, side).start()
        mine = dot(select[4], terms)
        return [backs[b] + mine[b * samples : (b + 1) * samples] for b in range(slots)]

    def take_back(k, parts):
        total = list(parts)
        for up, side in near[4:] + near[2:4] + near[:2]:
            back_arrival(k, up, side).wait_recv()
            for b in range(slots):
                piece = arrive[k, at(up, side), b * samples : (b + 1) * samples]
                total[b] = total[b] + piece.astype(jnp.float32)
        return total

    diagonal = lax.broadcasted_iota(jnp.int32, (samples, LANES), 1) - lax.broadcasted_iota(
        jnp.int32, (samples, LANES), 0
    )

    def inner(first, second):
        total = first[0] * second[0]
        for b in range(1, slots):
            total = total + first[b] * second[b]
        return jnp.sum(total, axis=1, keepdims=True)

    def row_copy(k, step):
        here = row_sum.at[k, ring]
        return remote(here, here, row_send.at[k], row_recv.at[k], row_mate(step))

    def col_copy(k, step):
        here = col_sum.at[k, block]
        return remote(here, here, col_send.at[k], col_recv.at[k], col_mate(step))

    def sum_first(k, columns):
        packed = jnp.zeros((samples, LANES), jnp.float32)
        for i, column in enumerate(columns):
            packed = packed + jnp.where(diagonal == i * samples, column, 0.0)
        col_sum[k, block] = jnp.sum(packed, axis=0, keepdims=True)
        for step in far_first(cols):
            col_copy(k, step).start()

    def sum_second(k):
        many = col_sum.at[k, pl.ds(0, cols - 1)]
        remote(many, many, col_send.at[k], col_recv.at[k], col_mate(1)).wait_recv()
        row_sum[k, ring] = jnp.sum(col_sum[k], axis=0)
        for step in far_first(row):
            row_copy(k, step).start()

    def sum_last(k, n):
        many = row_sum.at[k, pl.ds(0, row - 1)]
        remote(many, many, row_send.at[k], row_recv.at[k], row_mate(1)).wait_recv()
        total = jnp.broadcast_to(jnp.sum(row_sum[k], axis=0), (samples, LANES))
        return [
            jnp.sum(jnp.where(diagonal == i * samples, total, 0.0), axis=1, keepdims=True)
            for i in range(n)
        ]

    def sums_sent(k):
        many = row_sum.at[k, pl.ds(0, row - 1)]
        remote(many, many, row_send.at[k], row_recv.at[k], row_mate(1)).wait_send()
        many = col_sum.at[k, pl.ds(0, cols - 1)]
        remote(many, many, col_send.at[k], col_recv.at[k], col_mate(1)).wait_send()

    for load in loads[:3]:
        load.wait()
    each = range(slots)
    live = [jnp.where(b < count_ref[0, 0], 1.0, 0.0).astype(jnp.float32) for b in range(slots)]
    source = [rhs[b] * live[b] for b in each]
    scale = [pre[b] for b in each]
    first = [scale[b] * source[b] for b in each]
    pl.semaphore_wait(barrier, len(near) + len(close) + len(mates))
    send_field(0, first)
    if handed:
        tell(far_col.at[0], block_mate(0, lats // 4, 0))
        tell(far_col.at[0], block_mate(0, 0, wide // 2))
        tell(far_row.at[0], row_mate(REACH))
        tell(far_row.at[0], row_mate(row - REACH))

    loads[3].wait()
    loads[4].wait()

    wanted = []
    for b in range(slots):
        for m in range(links):
            position = owner_ref[near_ref[m, b]]
            region = position // slots
            slot = position - region * slots
            region_lat = region // lons
            up = region_lat - lat
            side = lax.rem(region - region_lat * lons - lon + 1 + lons, lons)
            index = ((up + 1) * 3 + side) * slots + slot
            wanted.append(jnp.clip(index, 0, 9 * slots - 1))
    depth = slots * links * samples
    lane = lax.broadcasted_iota(jnp.int32, (1, depth), 1)
    link, sample = lane // samples, lane % samples
    goal = sample
    for i, w in enumerate(wanted):
        goal = goal + jnp.where(link == i, w * samples, 0)
    for r in range(9):
        rows = lax.broadcasted_iota(jnp.int32, (high, depth), 0) + r * high
        select[r] = jnp.where(rows == goal, 1.0, 0.0).astype(jnp.bfloat16)

    loads[5].wait()
    for b in each:
        for m in range(links):
            turned_kri[b, m] = kri[b, m].T
    loads[6].wait()
    for b in each:
        turned_fac[b] = fac[b].T

    away = gather(0)
    if handed:
        pl.semaphore_wait(far_row.at[0], 2)
        tell(far_row.at[1], row_mate(2 * REACH))
        tell(far_row.at[1], row_mate(row - 2 * REACH))
    white = whiten([first[b].astype(jnp.bfloat16).astype(jnp.float32) - away[b] for b in each])
    for b in each:
        whitened[b] = white[b]
    columns = [inner(source, first), inner(white, white) + inner(first, first)]

    def early_sum():
        if handed:
            pl.semaphore_wait(far_col.at[0], 2)
        sum_first(0, columns)

    image = send_back(0, white, early_sum)
    if handed:
        pl.semaphore_wait(far_row.at[1], 2)
    sum_second(0)
    image = take_back(0, image)
    image = [image[b] + first[b] for b in each]

    scaled = [scale[b] * image[b] for b in each]
    send_field(1, scaled)
    slope_seen = inner(first, image)
    away = gather(1)
    current, slope = sum_last(0, 2)
    alpha = current / slope
    parts = [
        alpha * (scaled[b].astype(jnp.bfloat16).astype(jnp.float32) - away[b]) for b in each
    ]
    white = whiten(parts)
    scaled = [alpha * scaled[b] for b in each]
    even = [alpha * white[b] for b in each]
    less = [alpha * scaled[b] for b in each]
    columns = [
        slope_seen,
        inner([alpha * image[b] for b in each], scaled),
        inner([whitened[b] for b in each], even) + inner(first, less),
        inner(white, even) + inner(scaled, less),
    ]
    sum_first(1, columns)
    turned = send_back(1, white)
    sum_second(1)
    turned = take_back(1, turned)
    for b in each:
        first_ref[b] = first[b]
        scaled_ref[b] = scaled[b]
        source_ref[b] = source[b]
        image_ref[b] = image[b]
        turned_ref[b] = turned[b] + scaled[b]
    for k in range(2):
        for up, side in near:
            halo_copy(k, up, side).wait_send()
            back_copy(k, up, side).wait_send()
        for side in (-1, 1):
            halo_relay(k, side).wait_send()
            back_relay(k, side).wait_send()
    sums_sent(0)
    slope_seen, bend, mixed, last = sum_last(1, 4)
    following = current - 2.0 * (alpha * slope_seen) + bend
    grown = 1.0 + following / current
    step_size = alpha * (following / (grown * (grown * current - 2.0 * mixed) + last))
    along_ref[...] = jnp.broadcast_to(alpha + step_size * grown, (samples, width))
    step_ref[...] = jnp.broadcast_to(step_size, (samples, width))
    sums_sent(1)


def body(row, rhs, precond, factor, kriging, neighbours, owner, counts):
    slots, links, width = kriging.shape[2], kriging.shape[3], kriging.shape[4]
    samples = rhs.shape[3]
    lats, lons = lax.axis_size("lat"), lax.axis_size("lon")
    cols = lats * (lons // row)
    high = slots * samples
    field = jax.ShapeDtypeStruct((slots, samples, width), jnp.float32)
    far = pl.BlockSpec(memory_space=pl.ANY)
    vmem = pl.BlockSpec(memory_space=pltpu.VMEM)
    first, scaled, source, image, turned, along, step_size = pl.pallas_call(
        functools.partial(kernel, (lats, lons, row)),
        out_shape=(field,) * 5 + (jax.ShapeDtypeStruct((samples, width), jnp.float32),) * 2,
        in_specs=[far] * 7,
        out_specs=(vmem,) * 7,
        scratch_shapes=[
            pltpu.VMEM((slots, samples, width), jnp.float32),
            pltpu.VMEM((slots, 1, width), jnp.float32),
            pltpu.VMEM((slots, width, width), jnp.bfloat16),
            pltpu.VMEM((slots, links, width, width), jnp.bfloat16),
            pltpu.SMEM((links, slots), jnp.int32),
            pltpu.SMEM(owner.shape, jnp.int32),
            pltpu.SMEM((1, 1), jnp.int32),
            pltpu.VMEM((slots, links, width, width), jnp.bfloat16),
            pltpu.VMEM((slots, width, width), jnp.bfloat16),
            pltpu.VMEM((slots, samples, width), jnp.float32),
            pltpu.VMEM((2, 9 * slots, samples, width), jnp.bfloat16),
            pltpu.VMEM((slots * links * samples, width), jnp.bfloat16),
            pltpu.VMEM((9, high, slots * links * samples), jnp.bfloat16),
            pltpu.VMEM((2, 9, high, width), jnp.bfloat16),
            pltpu.VMEM((2, 9, high, width), jnp.bfloat16),
            pltpu.VMEM((2, 2, high, width), jnp.bfloat16),
            pltpu.VMEM((2, row, 1, LANES), jnp.float32),
            pltpu.VMEM((2, cols, 1, LANES), jnp.float32),
            pltpu.SemaphoreType.DMA((7,)),
            pltpu.SemaphoreType.DMA((2, 9)),
            pltpu.SemaphoreType.DMA((2, 9)),
            pltpu.SemaphoreType.DMA((2, 9)),
            pltpu.SemaphoreType.DMA((2, 9)),
            pltpu.SemaphoreType.DMA((2, 2)),
            pltpu.SemaphoreType.DMA((2, 2)),
            pltpu.SemaphoreType.REGULAR((1,)),
            pltpu.SemaphoreType.REGULAR((2,)),
            pltpu.SemaphoreType.DMA((2,)),
            pltpu.SemaphoreType.DMA((2,)),
            pltpu.SemaphoreType.DMA((2,)),
            pltpu.SemaphoreType.DMA((2,)),
        ],
        compiler_params=pltpu.CompilerParams(
            collective_id=0, has_side_effects=True, vmem_limit_bytes=32 * 2**20
        ),
    )(
        *(
            pltpu.with_memory_space_constraint(a, pltpu.HBM)
            for a in (
                rhs[0, 0], precond.reshape(slots, 1, width), factor[0, 0], kriging[0, 0],
                neighbours[0, 0].T, owner,
            )
        ),
        counts,
    )
    solved = along * first - step_size * scaled
    left = source - along * image + step_size * turned
    return solved[None, None], left[None, None]


def solution(mesh):
    lons = mesh.shape["lon"]
    row = ROW if lons % ROW == 0 else 2
    return jax.shard_map(
        functools.partial(body, row),
        mesh=mesh,
        in_specs=(
            P("lat", "lon", None, None, None),
            P("lat", "lon", None, None),
            P("lat", "lon", None, None, None),
            P("lat", "lon", None, None, None, None),
            P("lat", "lon", None, None),
            P(),
            P("lat", "lon"),
        ),
        out_specs=(P("lat", "lon", None, None, None), P("lat", "lon", None, None, None)),
        check_vma=False,
    )
```
